256 devices in a mesh: port: 4 (over z_hi), tile: 64 (over x, z_lo, y, core).
Axes of the slice: x: 4, y: 4, z: 8 (z_hi: 4, z_lo: 2; z = z_hi * 2 + z_lo), core: 2. Of those that a mesh axis runs over, the one named last changes fastest.
Arguments:
- e_start: float32 [4, 3, 1024, 4, 2048], P('port', None, 'tile'), may hold values from -6 to 6
- h_start: float32 [4, 3, 1024, 4, 2048], P('port', None, 'tile'), may hold values from -6 to 6
- forward: bfloat16 [4, 2, 2, 3, 1024, 4, 2048], P('port', None, None, None, 'tile'), may hold values from -6 to 6
- density: float32 [1024, 4, 2048], P('tile'), may hold values from 0 to 10
- material: int32 [1024, 4, 16], P('tile'), may hold values from 0 to 3
- design: int32 [1024, 4, 16], P('tile'), may hold values 0 or 1
- eps_table: float32 [4], replicated, may hold values from 1.5 to 12
- profiles: float32 [4, 2048], replicated, may hold values from -6 to 6
- port_mode: int32 [4], P('port'), may hold values from 0 to 3
Outputs:
- e_final: float32 [4, 3, 1024, 4, 2048], P('port', None, 'tile')
- h_final: float32 [4, 3, 1024, 4, 2048], P('port', None, 'tile')
- gradient: float32 [1024, 4, 2048], P('tile', 'port')
- intersections: float32 [4, 2, 2], P('port')
The draws below stay inside these ranges and needn't reach their ends.
All inputs are finite; a program needn't handle non-finite values. No bound on the sum of `design` on one device may be relied on, other than what follows from the above.
Results may differ from the reference program's by a relative error of at most 0.0003.
Values sent between devices are 32-bit elements; how exact they have to be, the bound alone decides.
No kernel may reach another device: no remote copies, remote signals or barrier semaphores. Data moves between devices by JAX's collectives and lax.ppermute only.
A program may use at most 128 MiB of HBM per device.

```python
import math
import jax
import jax.numpy as jnp
from jax import lax

PORTS = 4
NX = 1024
NZ = 4
NY = 2048
NYB = 16
STEPS = 16
NF = 2
MATS = 4
PROFILES = 4


def set_ends(values, rng, low, top_value):
    spot = [jax.random.randint(jax.random.fold_in(rng, axis), (), 0, length) for axis, length in enumerate(values.shape)]
    main_axis = values.shape.index(max(values.shape))
    beside = spot[:main_axis] + [(spot[main_axis] + 1) % values.shape[main_axis]] + spot[main_axis + 1:]
    return values.at[tuple(spot)].set(low).at[tuple(beside)].set(top_value)


def block_levels(stream_key, dims, cuts, smallest, largest):
    def one(dim, shards_of):
        draws = jax.random.uniform(jax.random.fold_in(jax.random.fold_in(stream_key, 6), dim), (shards_of,), jnp.float32, smallest / len(cuts), largest / len(cuts))
        return jnp.repeat(jnp.exp(draws), dims[dim] // shards_of).reshape((-1,) + (1,) * (len(dims) - dim - 1))

    gain = one(*cuts[0])
    for cut in cuts[1:]:
        gain = gain * one(*cut)
    return gain


def noise(stream_key, extent, spread, most, pieces=(), kind=jnp.bfloat16):
    drawn = jax.random.normal(stream_key, extent, jnp.float32) * spread
    if len(pieces) > 0:
        drawn = block_levels(stream_key, extent, pieces, -0.22, 0.18) * drawn
    return jnp.clip(drawn, min=-most, max=most).astype(kind)


def setup_inputs(seed: int = 0) -> dict:
    key_of = jax.random.split(jax.random.key(seed), 10)
    e_start = noise(key_of[0], (PORTS, 3, NX, NZ, NY), 1.0, 6.0, ((0, 4), (2, 64)), jnp.float32)
    h_start = noise(key_of[1], (PORTS, 3, NX, NZ, NY), 1.0, 6.0, ((0, 4), (2, 64)), jnp.float32)
    forward = noise(key_of[2], (PORTS, NF, 2, 3, NX, NZ, NY), 1.0, 6.0, ((0, 4), (4, 64)))
    density = jnp.clip(10.0 * jax.random.uniform(key_of[3], (NX, NZ, NY), jnp.float32) ** block_levels(key_of[3], (NX, NZ, NY), ((0, 64),), -0.2, 0.2), 0.0, 10.0)
    material = set_ends(jax.random.randint(key_of[4], (NX, NZ, NYB), 0, MATS), jax.random.fold_in(key_of[4], 1), 0, MATS - 1).astype(jnp.int32)
    design = set_ends((jax.random.randint(key_of[5], (NX, NZ, NYB), 0, 2) < 1).astype(jnp.int32), jax.random.fold_in(key_of[5], 1), 0, 1)
    eps_table = jnp.clip(jnp.exp(jax.random.uniform(key_of[6], (MATS,), jnp.float32, math.log(1.5), math.log(12.0))), 1.5, 12.0)
    profiles = noise(key_of[7], (PROFILES, NY), 1.0, 6.0, (), jnp.float32)
    port_mode = set_ends(jax.random.randint(key_of[8], (PORTS,), 0, PROFILES), jax.random.fold_in(key_of[8], 1), 0, PROFILES - 1).astype(jnp.int32)
    return dict(e_start=e_start, h_start=h_start, forward=forward, density=density, material=material, design=design, eps_table=eps_table, profiles=profiles, port_mode=port_mode)


OMEGA = 0.7
COEF_H = 0.5
COEF_E = 0.5

def shifted(field, axis, edge, ahead):
    count = field.shape[axis]
    if ahead:
        return jnp.concatenate([lax.slice_in_dim(field, 1, count, axis=axis), edge], axis=axis)
    return jnp.concatenate([edge, lax.slice_in_dim(field, 0, count - 1, axis=axis)], axis=axis)

def differ(field, axis, edge, ahead):
    axis = field.ndim + axis
    if edge is None:
        edge = jnp.zeros_like(lax.slice_in_dim(field, 0, 1, axis=axis))
    moved = shifted(field, axis, edge, ahead)
    if ahead:
        return moved - field
    return field - moved

def curl(field, edge_x, ahead):
    comp_x = field[..., 0, :, :, :]
    comp_y = field[..., 1, :, :, :]
    comp_z = field[..., 2, :, :, :]
    edge_y = None if edge_x is None else edge_x[..., 0, :, :, :]
    edge_z = None if edge_x is None else edge_x[..., 1, :, :, :]
    curl_x = differ(comp_z, -1, None, ahead) - differ(comp_y, -2, None, ahead)
    curl_y = differ(comp_x, -2, None, ahead) - differ(comp_z, -3, edge_z, ahead)
    curl_z = differ(comp_y, -3, edge_y, ahead) - differ(comp_x, -1, None, ahead)
    return jnp.stack([curl_x, curl_y, curl_z], axis=-4)

def reference(e_start, h_start, forward, density, material, design, eps_table, profiles, port_mode):
    mat_cells = jnp.repeat(material, 128, axis=2)
    design_cells = jnp.repeat(design, 128, axis=2).astype(jnp.float32)
    eps = eps_table[mat_cells] + design_cells * density
    omegas = OMEGA * (jnp.arange(NF) + 1).astype(jnp.float32)
    total = jnp.zeros(density.shape, jnp.float32)
    e_list = []
    h_list = []
    over_list = []
    for port in range(PORTS):

        def advance(step, carry):
            e_now, h_now, acc_re, acc_im = carry
            h_now = h_now - COEF_H * curl(e_now, None, True)
            e_now = e_now + COEF_E / eps * curl(h_now, None, False)
            moment = (step + 1).astype(jnp.float32)
            cosine = jnp.cos(omegas * moment)[:, None, None, None, None]
            sine = jnp.sin(omegas * moment)[:, None, None, None, None]
            acc_re = acc_re + cosine * e_now[None]
            acc_im = acc_im - sine * e_now[None]
            return (e_now, h_now, acc_re, acc_im)
        zeros = jnp.zeros((NF,) + e_start.shape[1:], jnp.float32)
        e_now, h_now, acc_re, acc_im = lax.fori_loop(0, STEPS, advance, (e_start[port], h_start[port], zeros, zeros))
        fields = forward[port].astype(jnp.float32)
        total = total + lax.optimization_barrier(jnp.sum(fields[:, 0] * acc_re - fields[:, 1] * acc_im, axis=(0, 1)))
        profile = profiles[port_mode[port]]
        over_re = lax.optimization_barrier(jnp.sum(acc_re[:, 1] * profile, axis=(1, 2, 3)))
        over_im = lax.optimization_barrier(jnp.sum(acc_im[:, 1] * profile, axis=(1, 2, 3)))
        over_list.append(jnp.stack([over_re, over_im], axis=-1) / math.sqrt(NX * NZ * NY))
        e_list.append(e_now)
        h_list.append(h_now)
    gradient = design_cells * (total / STEPS)
    return (jnp.stack(e_list), jnp.stack(h_list), gradient, jnp.stack(over_list))
```

```python
import functools
import math

import jax
import jax.numpy as jnp
import numpy as np
from jax import lax
from jax.experimental import pallas as pl
from jax.experimental.pallas import tpu as pltpu
from jax.sharding import PartitionSpec as P

STEPS = 16
OMEGA = 0.7
COEF_H = 0.5
COEF_E = 0.5

WIDTH = 16
SLAB = 4
HALF = 2
DEPTH = STEPS // 2
FREQS = 2
CELLS = (SLAB, HALF, 8, 128)


def rows(x):
    lead = x.shape[:-2]
    x = x.reshape(lead + (SLAB, 16, 128))
    return jnp.swapaxes(x, -3, -2).reshape(lead + (64, 128))


def unrows(x):
    lead = x.shape[:-2]
    x = x.reshape(lead + (16, SLAB, 128))
    return jnp.swapaxes(x, -3, -2).reshape(lead + (SLAB, 2048))


def masks():
    lane = lax.broadcasted_iota(jnp.int32, (8, 128), 1)
    sub = lax.broadcasted_iota(jnp.int32, (8, 128), 0)
    return lane == 127, lane == 0, sub == 7, sub == 0


def ahead_y(pair, m):
    r0 = pltpu.roll(pair[0], 127, 1)
    r1 = pltpu.roll(pair[1], 127, 1)
    rs = jnp.where(m[2], 0.0, pltpu.roll(r0, 7, 0))
    return jnp.where(m[0], r1, r0), jnp.where(m[0], rs, r1)


def behind_y(pair, m):
    r0 = pltpu.roll(pair[0], 1, 1)
    r1 = pltpu.roll(pair[1], 1, 1)
    rs = jnp.where(m[3], 0.0, pltpu.roll(r1, 1, 0))
    return jnp.where(m[1], rs, r0), jnp.where(m[1], r0, r1)


def update_plane(e_old, e_next, h_now, h_prev, coef, e_new, m):
    def pair(ref, comp, z):
        return [ref[comp, z, v] for v in range(HALF)]

    ex, ey = pair(e_old, 0, 0), pair(e_old, 1, 0)
    below = None
    for z in range(SLAB):
        ez = pair(e_old, 2, z)
        ex_up = pair(e_old, 0, z + 1) if z + 1 < SLAB else [0.0, 0.0]
        ey_up = pair(e_old, 1, z + 1) if z + 1 < SLAB else [0.0, 0.0]
        ey_x, ez_x = pair(e_next, 1, z), pair(e_next, 2, z)
        ez_y, ex_y = ahead_y(ez, m), ahead_y(ex, m)
        hx, hy, hz = pair(h_now, 0, z), pair(h_now, 1, z), pair(h_now, 2, z)
        for v in range(HALF):
            hx[v] = hx[v] - ((ez_y[v] - ez[v]) - (ey_up[v] - ey[v]))
            hy[v] = hy[v] - ((ex_up[v] - ex[v]) - (ez_x[v] - ez[v]))
            hz[v] = hz[v] - ((ey_x[v] - ey[v]) - (ex_y[v] - ex[v]))
            h_now[0, z, v] = hx[v]
            h_now[1, z, v] = hy[v]
            h_now[2, z, v] = hz[v]
        hz_y, hx_y = behind_y(hz, m), behind_y(hx, m)
        hy_x, hz_x = pair(h_prev, 1, z), pair(h_prev, 2, z)
        hx_z, hy_z = below if z > 0 else ([0.0, 0.0], [0.0, 0.0])
        for v in range(HALF):
            c = coef[z, v]
            e_new[0, z, v] = ex[v] + c * ((hz[v] - hz_y[v]) - (hy[v] - hy_z[v]))
            e_new[1, z, v] = ey[v] + c * ((hx[v] - hx_z[v]) - (hz[v] - hz_x[v]))
            e_new[2, z, v] = ez[v] + c * ((hy[v] - hy_x[v]) - (hx[v] - hx_y[v]))
        ex, ey, below = ex_up, ey_up, (hx, hy)


def strided(z, v):
    return pl.ds(4 * v + z, 8, stride=8)


def load_rows(src, dst, dst_base, scale):
    def one(x, _):
        for comp in range(3):
            for z in range(SLAB):
                for v in range(HALF):
                    val = src[comp, x, strided(z, v), :]
                    dst[comp, dst_base + x, z, v] = val if scale == 1.0 else val * scale
        return 0

    lax.fori_loop(0, WIDTH, one, 0)


def coef_kernel(table, mat, des, dens, coef, mask):
    kind = mat[...]
    base = jnp.zeros((8, 128), jnp.float32)
    for which in range(table.shape[0]):
        base = base + jnp.where(kind == which, table[which], 0.0)
    flag = des[...].astype(jnp.float32)
    for x in range(WIDTH):
        for z in range(SLAB):
            for v in range(HALF):
                at = (x * SLAB + z) * HALF + v
                b = jnp.broadcast_to(base[:, at : at + 1], (8, 128))
                d = jnp.broadcast_to(flag[:, at : at + 1], (8, 128))
                eps = b + d * dens[x, strided(z, v), :]
                coef[x, z, v] = (COEF_E * COEF_H) / eps
                mask[x, z, v] = d * (1.0 / STEPS)


def free_kernel(e_in, h_in, coef, hist_e, hist_h, e, h):
    m = masks()
    load_rows(e_in, e, 0, 1.0)
    load_rows(h_in, h, 1, 1.0 / COEF_H)
    e[:, WIDTH] = jnp.zeros((3,) + CELLS, jnp.float32)
    h[:, 0] = jnp.zeros((3,) + CELLS, jnp.float32)
    hist_e[0] = e[1:3, 0]

    def sweep(low, high):
        def one(x, _):
            update_plane(e.at[:, x], e.at[:, x + 1], h.at[:, x + 1], h.at[:, x], coef.at[x], e.at[:, x], m)
            return 0

        lax.fori_loop(low, high, one, 0)

    def early(s, _):
        sweep(0, WIDTH)
        hist_e[s] = e[1:3, 0]
        hist_h[s - 1] = h[1:3, WIDTH]
        return 0

    def late(s, _):
        sweep(0, WIDTH - s)
        sweep(s - 1, WIDTH)

        @pl.when(s < STEPS)
        def _():
            hist_e[s] = e[1:3, 0]

        hist_h[s - 1] = h[1:3, WIDTH]
        return 0

    lax.fori_loop(1, DEPTH + 1, early, 0)
    lax.fori_loop(DEPTH + 1, STEPS + 1, late, 0)


def full_kernel(
    info, e_in, h_in, coef, coef_l, coef_r, got_e, got_h, forward, mask, profile,
    e_out, h_out, grad, over,
    e, h, el, hl, er, hr, wide, sums,
):
    m = masks()
    load_rows(e_in, e.at[0], 0, 1.0)
    load_rows(h_in, h, 1, 1.0 / COEF_H)
    for ref in (el, hl, er, hr):
        ref[...] = jnp.zeros(ref.shape, jnp.float32)
    inner = (info[0] > 0).astype(jnp.float32)

    def step(s, _):
        before, after = e.at[s - 1], e.at[s]
        n_left = jnp.minimum(s, STEPS + 1 - s)
        n_right = jnp.minimum(s, STEPS - s)
        el[1:3, DEPTH + 1] = before[1:3, 0]
        before[1:3, WIDTH] = er[1:3, 0] + got_e[s - 1]

        def left(x, _):
            update_plane(el.at[:, x], el.at[:, x + 1], hl.at[:, x], hl.at[:, x - 1], coef_l.at[x - 1], el.at[:, x], m)
            return 0

        lax.fori_loop(DEPTH + 1 - n_left, DEPTH + 1, left, 0)
        h[1:3, 0] = hl[1:3, DEPTH] * inner + got_h[s - 1]

        def own(x, _):
            update_plane(before.at[:, x], before.at[:, x + 1], h.at[:, x + 1], h.at[:, x], coef.at[x], after.at[:, x], m)
            return 0

        lax.fori_loop(0, WIDTH, own, 0)
        hr[1:3, 0] = h[1:3, WIDTH]

        def right(x, _):
            update_plane(er.at[:, x], er.at[:, x + 1], hr.at[:, x + 1], hr.at[:, x], coef_r.at[x], er.at[:, x], m)
            return 0

        lax.fori_loop(0, n_right, right, 0)
        return 0

    lax.fori_loop(1, STEPS + 1, step, 0)

    port = info[1]
    omegas = [OMEGA * (f + 1) for f in range(FREQS)]
    mid = (STEPS + 1) / 2
    ca = [float(np.cos(w * mid)) for w in omegas]
    sa = [float(np.sin(w * mid)) for w in omegas]
    sums[...] = jnp.zeros(sums.shape, jnp.float32)

    def finish(x, _):
        for f in range(FREQS):
            for q in range(2):
                for comp in range(3):
                    wide[(f * 2 + q) * 3 + comp] = forward[f, q, comp, x].astype(jnp.float32)
        for z in range(SLAB):
            for v in range(HALF):
                total = None
                for comp in range(3):
                    plus, minus = [], []
                    for i in range(STEPS // 2):
                        lo = e[STEPS // 2 - i, comp, x, z, v]
                        hi = e[STEPS // 2 + 1 + i, comp, x, z, v]
                        plus.append(hi + lo)
                        minus.append(hi - lo)
                    for f in range(FREQS):
                        even = odd = None
                        for i in range(STEPS // 2):
                            c = float(np.cos(omegas[f] * (i + 0.5)))
                            s = float(np.sin(omegas[f] * (i + 0.5)))
                            even = c * plus[i] if even is None else even + c * plus[i]
                            odd = s * minus[i] if odd is None else odd + s * minus[i]
                        if comp == 1:
                            sums[f, 0, v] += even
                            sums[f, 1, v] += odd
                        re = wide[(f * 2) * 3 + comp, strided(z, v), :]
                        im = wide[(f * 2 + 1) * 3 + comp, strided(z, v), :]
                        term = even * (re * ca[f] + im * sa[f]) + odd * (im * ca[f] - re * sa[f])
                        total = term if total is None else total + term
                grad[lax.rem(z - port + SLAB, SLAB), x, v] = mask[x, z, v] * total
                for comp in range(3):
                    e_out[comp, x, strided(z, v), :] = e[STEPS, comp, x, z, v]
                    h_out[comp, x, strided(z, v), :] = h[comp, x + 1, z, v] * COEF_H
        return 0

    lax.fori_loop(0, WIDTH, finish, 0)
    for f in range(FREQS):
        even = sum(sums[f, 0, v] * profile[info[2], v] for v in range(HALF))
        odd = sum(sums[f, 1, v] * profile[info[2], v] for v in range(HALF))
        re = ca[f] * even - sa[f] * odd
        im = -(sa[f] * even + ca[f] * odd)
        for q, val in enumerate((re, im)):
            val = jnp.sum(jnp.sum(val, axis=0, keepdims=True), axis=1, keepdims=True)
            over[2 * f + q : 2 * f + q + 1, :] = jnp.broadcast_to(val, (1, 128))


def sum_kernel(a, b, c, d, out):
    for x in range(WIDTH):
        for v in range(HALF):
            out[x, pl.ds(v, 8, stride=2), :] = (a[x, v] + b[x, v]) + (c[x, v] + d[x, v])


def f32(*shape):
    return jax.ShapeDtypeStruct(shape, jnp.float32)


VMEM = pl.BlockSpec(memory_space=pltpu.VMEM)
SMEM = pl.BlockSpec(memory_space=pltpu.SMEM)
PARAMS = pltpu.CompilerParams(vmem_limit_bytes=58 * 1024 * 1024)


def body(e_start, h_start, forward, density, material, design, eps_table, profiles, port_mode):
    tiles = lax.axis_size("tile")
    ports = lax.axis_size("port")
    tile = lax.axis_index("tile")
    port = lax.axis_index("port")
    to_right = [(i, i + 1) for i in range(tiles - 1)]
    to_left = [(i + 1, i) for i in range(tiles - 1)]

    def by_sublane(x):
        return x.reshape(WIDTH * SLAB, 8, HALF).transpose(1, 0, 2).reshape(8, 128)

    coef, mask = pl.pallas_call(
        coef_kernel,
        out_shape=(f32(WIDTH, *CELLS), f32(WIDTH, *CELLS)),
        in_specs=[SMEM, VMEM, VMEM, VMEM],
        out_specs=(VMEM, VMEM),
        name="coef",
    )(eps_table, by_sublane(material), by_sublane(design), rows(density))
    coef_l = lax.ppermute(coef[WIDTH - DEPTH :], "tile", to_right)
    coef_r = lax.ppermute(coef[:DEPTH], "tile", to_left)

    e_rows, h_rows = rows(e_start[0]), rows(h_start[0])
    hist_e, hist_h = pl.pallas_call(
        free_kernel,
        out_shape=(f32(STEPS, 2, *CELLS), f32(STEPS, 2, *CELLS)),
        in_specs=[VMEM] * 3,
        out_specs=(VMEM, VMEM),
        scratch_shapes=[pltpu.VMEM((3, WIDTH + 1) + CELLS, jnp.float32)] * 2,
        compiler_params=PARAMS,
        name="free",
    )(e_rows, h_rows, coef)
    got_e = lax.ppermute(hist_e, "tile", to_left)
    got_h = lax.ppermute(hist_h, "tile", to_right)

    info = jnp.stack([tile.astype(jnp.int32), port.astype(jnp.int32), port_mode[0]])
    profile = profiles.reshape(-1, 8, HALF, 128).transpose(0, 2, 1, 3)
    e_out, h_out, grad, over = pl.pallas_call(
        full_kernel,
        out_shape=(
            f32(3, WIDTH, 64, 128),
            f32(3, WIDTH, 64, 128),
            f32(SLAB, WIDTH, HALF, 8, 128),
            f32(2 * FREQS, 128),
        ),
        in_specs=[SMEM] + [VMEM] * 10,
        out_specs=(VMEM,) * 4,
        scratch_shapes=[
            pltpu.VMEM((STEPS + 1, 3, WIDTH + 1) + CELLS, jnp.float32),
            pltpu.VMEM((3, WIDTH + 1) + CELLS, jnp.float32),
            pltpu.VMEM((3, DEPTH + 2) + CELLS, jnp.float32),
            pltpu.VMEM((3, DEPTH + 1) + CELLS, jnp.float32),
            pltpu.VMEM((3, DEPTH + 1) + CELLS, jnp.float32),
            pltpu.VMEM((3, DEPTH + 1) + CELLS, jnp.float32),
            pltpu.VMEM((4 * 3, 64, 128), jnp.float32),
            pltpu.VMEM((FREQS, 2, HALF, 8, 128), jnp.float32),
        ],
        compiler_params=PARAMS,
        name="full",
    )(info, e_rows, h_rows, coef, coef_l, coef_r, got_e, got_h, rows(forward[0]), mask, profile)

    parts = [grad[0]]
    for d in range(1, ports):
        parts.append(lax.ppermute(grad[d], "port", [(i, (i + d) % ports) for i in range(ports)]))
    total = over
    span = 1
    while span < tiles:
        radix = min(4, tiles // span)
        got = []
        for d in range(1, radix):
            pairs = []
            for i in range(tiles):
                digit = i // span % radix
                pairs.append((i, i + ((digit + d) % radix - digit) * span))
            got.append(lax.ppermute(total, "tile", pairs))
        total = total + sum(got[1:], got[0])
        span *= radix
    gradient = pl.pallas_call(
        sum_kernel,
        out_shape=f32(WIDTH, 16, 128),
        in_specs=[VMEM] * 4,
        out_specs=VMEM,
        name="total",
    )(*parts)
    scale = math.sqrt(WIDTH * tiles * SLAB * 2048)
    intersections = (total[:, 0] / scale).reshape(1, FREQS, 2)
    return (
        unrows(e_out)[None],
        unrows(h_out)[None],
        gradient.reshape(WIDTH, 1, 2048),
        intersections,
    )


def solution(mesh):
    return jax.shard_map(
        body,
        mesh=mesh,
        in_specs=(
            P("port", None, "tile", None, None),
            P("port", None, "tile", None, None),
            P("port", None, None, None, "tile", None, None),
            P("tile", None, None),
            P("tile", None, None),
            P("tile", None, None),
            P(),
            P(),
            P("port"),
        ),
        out_specs=(
            P("port", None, "tile", None, None),
            P("port", None, "tile", None, None),
            P("tile", "port", None),
            P("port", None, None),
        ),
        check_vma=False,
    )
```

```python
import functools
import math

import jax
import jax.numpy as jnp
import numpy as np
from jax import lax
from jax.experimental import pallas as pl
from jax.experimental.pallas import tpu as pltpu
from jax.sharding import PartitionSpec as P

STEPS = 16
OMEGA = 0.7
COEF_H = 0.5
COEF_E = 0.5

WIDTH = 16
SLAB = 4
HALF = 2
DEPTH = STEPS // 2
FREQS = 2
CELLS = (SLAB, HALF, 8, 128)


def rows(x):
    lead = x.shape[:-2]
    x = x.reshape(lead + (SLAB, 16, 128))
    return jnp.swapaxes(x, -3, -2).reshape(lead + (64, 128))


def unrows(x):
    lead = x.shape[:-2]
    x = x.reshape(lead + (16, SLAB, 128))
    return jnp.swapaxes(x, -3, -2).reshape(lead + (SLAB, 2048))


def masks():
    lane = lax.broadcasted_iota(jnp.int32, (8, 128), 1)
    sub = lax.broadcasted_iota(jnp.int32, (8, 128), 0)
    return lane == 127, lane == 0, sub == 7, sub == 0


def ahead_y(pair, m):
    r0 = pltpu.roll(pair[0], 127, 1)
    r1 = pltpu.roll(pair[1], 127, 1)
    rs = jnp.where(m[2], 0.0, pltpu.roll(r0, 7, 0))
    return jnp.where(m[0], r1, r0), jnp.where(m[0], rs, r1)


def behind_y(pair, m):
    r0 = pltpu.roll(pair[0], 1, 1)
    r1 = pltpu.roll(pair[1], 1, 1)
    rs = jnp.where(m[3], 0.0, pltpu.roll(r1, 1, 0))
    return jnp.where(m[1], rs, r0), jnp.where(m[1], r0, r1)


def update_plane(e_old, e_next, h_now, h_prev, coef, e_new, m):
    def plane(ref, comp):
        return [[ref[comp, z, v] for v in range(HALF)] for z in range(SLAB)]

    ex, ey, ez = (plane(e_old, comp) for comp in range(3))
    ey_x, ez_x = plane(e_next, 1), plane(e_next, 2)
    hx, hy, hz = (plane(h_now, comp) for comp in range(3))
    hy_x, hz_x = plane(h_prev, 1), plane(h_prev, 2)
    c = [[coef[z, v] for v in range(HALF)] for z in range(SLAB)]
    edge = [0.0] * HALF
    new_e = []
    for z in range(SLAB):
        ex_z, ey_z = (ex[z + 1], ey[z + 1]) if z + 1 < SLAB else (edge, edge)
        ez_y, ex_y = ahead_y(ez[z], m), ahead_y(ex[z], m)
        for v in range(HALF):
            hx[z][v] = hx[z][v] - ((ez_y[v] - ez[z][v]) - (ey_z[v] - ey[z][v]))
            hy[z][v] = hy[z][v] - ((ex_z[v] - ex[z][v]) - (ez_x[z][v] - ez[z][v]))
            hz[z][v] = hz[z][v] - ((ey_x[z][v] - ey[z][v]) - (ex_y[v] - ex[z][v]))
        hz_y, hx_y = behind_y(hz[z], m), behind_y(hx[z], m)
        hx_z, hy_z = (hx[z - 1], hy[z - 1]) if z > 0 else (edge, edge)
        for v in range(HALF):
            curl_x = (hz[z][v] - hz_y[v]) - (hy[z][v] - hy_z[v])
            curl_y = (hx[z][v] - hx_z[v]) - (hz[z][v] - hz_x[z][v])
            curl_z = (hy[z][v] - hy_x[z][v]) - (hx[z][v] - hx_y[v])
            new_e.append(
                (
                    ex[z][v] + c[z][v] * curl_x,
                    ey[z][v] + c[z][v] * curl_y,
                    ez[z][v] + c[z][v] * curl_z,
                )
            )
    for z in range(SLAB):
        for v in range(HALF):
            for comp, h in enumerate((hx, hy, hz)):
                h_now[comp, z, v] = h[z][v]
                e_new[comp, z, v] = new_e[z * HALF + v][comp]


def sweep(first, last, one):
    def four(i, _):
        for k in range(4):
            one(4 * i + k)
        return 0

    lax.fori_loop(first, last, four, 0)


def strided(z, v):
    return pl.ds(4 * v + z, 8, stride=8)


def load_rows(src, dst, dst_base, scale):
    def one(x, _):
        for comp in range(3):
            for z in range(SLAB):
                for v in range(HALF):
                    val = src[comp, x, strided(z, v), :]
                    dst[comp, dst_base + x, z, v] = val if scale == 1.0 else val * scale
        return 0

    lax.fori_loop(0, WIDTH, one, 0)


def coef_kernel(table, mat, des, dens, coef, mask):
    kind = mat[...]
    base = jnp.zeros((8, 128), jnp.float32)
    for which in range(table.shape[0]):
        base = base + jnp.where(kind == which, table[which], 0.0)
    flag = des[...].astype(jnp.float32)
    for x in range(WIDTH):
        for z in range(SLAB):
            for v in range(HALF):
                at = (x * SLAB + z) * HALF + v
                b = jnp.broadcast_to(base[:, at : at + 1], (8, 128))
                d = jnp.broadcast_to(flag[:, at : at + 1], (8, 128))
                eps = b + d * dens[x, strided(z, v), :]
                coef[x, z, v] = (COEF_E * COEF_H) / eps
                mask[x, z, v] = d * (1.0 / STEPS)


def free_kernel(e_in, h_in, coef, hist_e, hist_h, e, h):
    m = masks()
    load_rows(e_in, e, 0, 1.0)
    load_rows(h_in, h, 1, 1.0 / COEF_H)
    e[:, WIDTH] = jnp.zeros((3,) + CELLS, jnp.float32)
    h[:, 0] = jnp.zeros((3,) + CELLS, jnp.float32)
    hist_e[0] = e[1:3, 0]

    def one(x):
        update_plane(e.at[:, x], e.at[:, x + 1], h.at[:, x + 1], h.at[:, x], coef.at[x], e.at[:, x], m)

    def early(s, _):
        sweep(0, WIDTH // 4, one)
        hist_e[s] = e[1:3, 0]
        hist_h[s - 1] = h[1:3, WIDTH]
        return 0

    def late(s, _):
        sweep(0, (WIDTH - s + 3) // 4, one)
        sweep((s - 1) // 4, WIDTH // 4, one)

        @pl.when(s < STEPS)
        def _():
            hist_e[s] = e[1:3, 0]

        hist_h[s - 1] = h[1:3, WIDTH]
        return 0

    lax.fori_loop(1, DEPTH + 1, early, 0)
    lax.fori_loop(DEPTH + 1, STEPS + 1, late, 0)


def full_kernel(
    info, e_in, h_in, coef, coef_l, coef_r, got_e, got_h, forward, mask, profile,
    e_out, h_out, grad, over,
    e, h, el, hl, er, hr, wide,
):
    m = masks()
    load_rows(e_in, e.at[0], 0, 1.0)
    load_rows(h_in, h, 1, 1.0 / COEF_H)
    for ref in (el, hl, er, hr):
        ref[...] = jnp.zeros(ref.shape, jnp.float32)
    inner = (info[0] > 0).astype(jnp.float32)

    def step(s, _):
        before, after = e.at[s - 1], e.at[s]
        n_left = jnp.minimum(s, STEPS + 1 - s)
        n_right = jnp.minimum(s, STEPS - s)
        el[1:3, DEPTH + 1] = before[1:3, 0]
        before[1:3, WIDTH] = er[1:3, 0] + got_e[s - 1]

        def left(x):
            update_plane(el.at[:, x + 1], el.at[:, x + 2], hl.at[:, x + 1], hl.at[:, x], coef_l.at[x], el.at[:, x + 1], m)

        sweep((DEPTH - n_left) // 4, DEPTH // 4, left)
        h[1:3, 0] = hl[1:3, DEPTH] * inner + got_h[s - 1]

        def own(x):
            update_plane(before.at[:, x], before.at[:, x + 1], h.at[:, x + 1], h.at[:, x], coef.at[x], after.at[:, x], m)

        sweep(0, WIDTH // 4, own)
        hr[1:3, 0] = h[1:3, WIDTH]

        def right(x):
            update_plane(er.at[:, x], er.at[:, x + 1], hr.at[:, x + 1], hr.at[:, x], coef_r.at[x], er.at[:, x], m)

        sweep(0, (n_right + 3) // 4, right)
        return 0

    lax.fori_loop(1, STEPS + 1, step, 0)

    port = info[1]
    omegas = [OMEGA * (f + 1) for f in range(FREQS)]
    mid = (STEPS + 1) / 2
    ca = [float(np.cos(w * mid)) for w in omegas]
    sa = [float(np.sin(w * mid)) for w in omegas]

    def finish(x, acc):
        for f in range(FREQS):
            for q in range(2):
                for comp in range(3):
                    wide[(f * 2 + q) * 3 + comp] = forward[f, q, comp, x].astype(jnp.float32)

        def at_z(z, acc):
            acc = list(acc)
            for v in range(HALF):
                total = None
                for comp in range(3):
                    plus, minus = [], []
                    for i in range(STEPS // 2):
                        lo = e[STEPS // 2 - i, comp, x, z, v]
                        hi = e[STEPS // 2 + 1 + i, comp, x, z, v]
                        plus.append(hi + lo)
                        minus.append(hi - lo)
                    for f in range(FREQS):
                        even = odd = None
                        for i in range(STEPS // 2):
                            c = float(np.cos(omegas[f] * (i + 0.5)))
                            s = float(np.sin(omegas[f] * (i + 0.5)))
                            even = c * plus[i] if even is None else even + c * plus[i]
                            odd = s * minus[i] if odd is None else odd + s * minus[i]
                        if comp == 1:
                            acc[(f * 2) * HALF + v] += even
                            acc[(f * 2 + 1) * HALF + v] += odd
                        re = wide[(f * 2) * 3 + comp, strided(z, v), :]
                        im = wide[(f * 2 + 1) * 3 + comp, strided(z, v), :]
                        term = even * (re * ca[f] + im * sa[f]) + odd * (im * ca[f] - re * sa[f])
                        total = term if total is None else total + term
                grad[lax.rem(z - port + SLAB, SLAB), x, v] = mask[x, z, v] * total
            return tuple(acc)

        acc = lax.fori_loop(0, SLAB, at_z, acc)

        def put(z, _):
            for v in range(HALF):
                for comp in range(3):
                    e_out[comp, x, strided(z, v), :] = e[STEPS, comp, x, z, v]
                    h_out[comp, x, strided(z, v), :] = h[comp, x + 1, z, v] * COEF_H
            return 0

        lax.fori_loop(0, SLAB, put, 0)
        return acc

    zero = jnp.zeros((8, 128), jnp.float32)
    acc = lax.fori_loop(0, WIDTH, finish, (zero,) * (FREQS * 2 * HALF))
    for f in range(FREQS):
        even = sum(acc[(f * 2) * HALF + v] * profile[info[2], v] for v in range(HALF))
        odd = sum(acc[(f * 2 + 1) * HALF + v] * profile[info[2], v] for v in range(HALF))
        re = ca[f] * even - sa[f] * odd
        im = -(sa[f] * even + ca[f] * odd)
        for q, val in enumerate((re, im)):
            val = jnp.sum(jnp.sum(val, axis=0, keepdims=True), axis=1, keepdims=True)
            over[2 * f + q : 2 * f + q + 1, :] = jnp.broadcast_to(val, (1, 128))


def sum_kernel(a, b, c, d, out):
    for x in range(WIDTH):
        for v in range(HALF):
            out[x, pl.ds(v, 8, stride=2), :] = (a[x, v] + b[x, v]) + (c[x, v] + d[x, v])


def f32(*shape):
    return jax.ShapeDtypeStruct(shape, jnp.float32)


VMEM = pl.BlockSpec(memory_space=pltpu.VMEM)
SMEM = pl.BlockSpec(memory_space=pltpu.SMEM)
PARAMS = pltpu.CompilerParams(vmem_limit_bytes=58 * 1024 * 1024)


def body(e_start, h_start, forward, density, material, design, eps_table, profiles, port_mode):
    tiles = lax.axis_size("tile")
    ports = lax.axis_size("port")
    tile = lax.axis_index("tile")
    port = lax.axis_index("port")
    to_right = [(i, i + 1) for i in range(tiles - 1)]
    to_left = [(i + 1, i) for i in range(tiles - 1)]

    def by_sublane(x):
        return x.reshape(WIDTH * SLAB, 8, HALF).transpose(1, 0, 2).reshape(8, 128)

    coef, mask = pl.pallas_call(
        coef_kernel,
        out_shape=(f32(WIDTH, *CELLS), f32(WIDTH, *CELLS)),
        in_specs=[SMEM, VMEM, VMEM, VMEM],
        out_specs=(VMEM, VMEM),
        name="coef",
    )(eps_table, by_sublane(material), by_sublane(design), rows(density))
    coef_l = lax.ppermute(coef[WIDTH - DEPTH :], "tile", to_right)
    coef_r = lax.ppermute(coef[:DEPTH], "tile", to_left)

    e_rows, h_rows = rows(e_start[0]), rows(h_start[0])
    hist_e, hist_h = pl.pallas_call(
        free_kernel,
        out_shape=(f32(STEPS, 2, *CELLS), f32(STEPS, 2, *CELLS)),
        in_specs=[VMEM] * 3,
        out_specs=(VMEM, VMEM),
        scratch_shapes=[pltpu.VMEM((3, WIDTH + 1) + CELLS, jnp.float32)] * 2,
        compiler_params=PARAMS,
        name="free",
    )(e_rows, h_rows, coef)
    got_e = lax.ppermute(hist_e, "tile", to_left)
    got_h = lax.ppermute(hist_h, "tile", to_right)

    info = jnp.stack([tile.astype(jnp.int32), port.astype(jnp.int32), port_mode[0]])
    profile = profiles.reshape(-1, 8, HALF, 128).transpose(0, 2, 1, 3)
    e_out, h_out, grad, over = pl.pallas_call(
        full_kernel,
        out_shape=(
            f32(3, WIDTH, 64, 128),
            f32(3, WIDTH, 64, 128),
            f32(SLAB, WIDTH, HALF, 8, 128),
            f32(2 * FREQS, 128),
        ),
        in_specs=[SMEM] + [VMEM] * 10,
        out_specs=(VMEM,) * 4,
        scratch_shapes=[
            pltpu.VMEM((STEPS + 1, 3, WIDTH + 1) + CELLS, jnp.float32),
            pltpu.VMEM((3, WIDTH + 1) + CELLS, jnp.float32),
            pltpu.VMEM((3, DEPTH + 2) + CELLS, jnp.float32),
            pltpu.VMEM((3, DEPTH + 1) + CELLS, jnp.float32),
            pltpu.VMEM((3, DEPTH + 1) + CELLS, jnp.float32),
            pltpu.VMEM((3, DEPTH + 1) + CELLS, jnp.float32),
            pltpu.VMEM((4 * 3, 64, 128), jnp.float32),
        ],
        compiler_params=PARAMS,
        name="full",
    )(info, e_rows, h_rows, coef, coef_l, coef_r, got_e, got_h, rows(forward[0]), mask, profile)

    parts = [grad[0]]
    for d in range(1, ports):
        parts.append(lax.ppermute(grad[d], "port", [(i, (i + d) % ports) for i in range(ports)]))
    total = over
    span = 1
    while span < tiles:
        radix = min(4, tiles // span)
        got = []
        for d in range(1, radix):
            pairs = []
            for i in range(tiles):
                digit = i // span % radix
                pairs.append((i, i + ((digit + d) % radix - digit) * span))
            got.append(lax.ppermute(total, "tile", pairs))
        total = total + sum(got[1:], got[0])
        span *= radix
    gradient = pl.pallas_call(
        sum_kernel,
        out_shape=f32(WIDTH, 16, 128),
        in_specs=[VMEM] * 4,
        out_specs=VMEM,
        name="total",
    )(*parts)
    scale = math.sqrt(WIDTH * tiles * SLAB * 2048)
    intersections = (total[:, 0] / scale).reshape(1, FREQS, 2)
    return (
        unrows(e_out)[None],
        unrows(h_out)[None],
        gradient.reshape(WIDTH, 1, 2048),
        intersections,
    )


def solution(mesh):
    return jax.shard_map(
        body,
        mesh=mesh,
        in_specs=(
            P("port", None, "tile", None, None),
            P("port", None, "tile", None, None),
            P("port", None, None, None, "tile", None, None),
            P("tile", None, None),
            P("tile", None, None),
            P("tile", None, None),
            P(),
            P(),
            P("port"),
        ),
        out_specs=(
            P("port", None, "tile", None, None),
            P("port", None, "tile", None, None),
            P("tile", "port", None),
            P("port", None, None),
        ),
        check_vma=False,
    )
```

```python
import functools
import math

import jax
import jax.numpy as jnp
import numpy as np
from jax import lax
from jax.experimental import pallas as pl
from jax.experimental.pallas import tpu as pltpu
from jax.sharding import PartitionSpec as P

STEPS = 16
OMEGA = 0.7
COEF_H = 0.5
COEF_E = 0.5

WIDTH = 16
SLAB = 4
HALF = 2
DEPTH = STEPS // 2
FREQS = 2
CELLS = (SLAB, HALF, 8, 128)


def rows(x):
    lead = x.shape[:-2]
    x = x.reshape(lead + (SLAB, 16, 128))
    return jnp.swapaxes(x, -3, -2).reshape(lead + (64, 128))


def unrows(x):
    lead = x.shape[:-2]
    x = x.reshape(lead + (16, SLAB, 128))
    return jnp.swapaxes(x, -3, -2).reshape(lead + (SLAB, 2048))


def masks():
    lane = lax.broadcasted_iota(jnp.int32, (8, 128), 1)
    sub = lax.broadcasted_iota(jnp.int32, (8, 128), 0)
    return lane == 127, lane == 0, sub == 7, sub == 0


def ahead_y(pair, m):
    r0 = pltpu.roll(pair[0], 127, 1)
    r1 = pltpu.roll(pair[1], 127, 1)
    rs = jnp.where(m[2], 0.0, pltpu.roll(r0, 7, 0))
    return jnp.where(m[0], r1, r0), jnp.where(m[0], rs, r1)


def behind_y(pair, m):
    r0 = pltpu.roll(pair[0], 1, 1)
    r1 = pltpu.roll(pair[1], 1, 1)
    rs = jnp.where(m[3], 0.0, pltpu.roll(r1, 1, 0))
    return jnp.where(m[1], rs, r0), jnp.where(m[1], r0, r1)


def update_plane(e_old, e_next, h_now, h_prev, coef, e_new, m, keep=None):
    def plane(ref, comp):
        return [[ref[comp, z, v] for v in range(HALF)] for z in range(SLAB)]

    ex, ey, ez = (plane(e_old, comp) for comp in range(3))
    ey_x, ez_x = plane(e_next, 1), plane(e_next, 2)
    hx, hy, hz = (plane(h_now, comp) for comp in range(3))
    hy_x, hz_x = plane(h_prev, 1), plane(h_prev, 2)
    c = [[coef[z, v] for v in range(HALF)] for z in range(SLAB)]
    edge = [0.0] * HALF
    new_e = []
    for z in range(SLAB):
        ex_z, ey_z = (ex[z + 1], ey[z + 1]) if z + 1 < SLAB else (edge, edge)
        ez_y, ex_y = ahead_y(ez[z], m), ahead_y(ex[z], m)
        for v in range(HALF):
            hx[z][v] = hx[z][v] - ((ez_y[v] - ez[z][v]) - (ey_z[v] - ey[z][v]))
            hy[z][v] = hy[z][v] - ((ex_z[v] - ex[z][v]) - (ez_x[z][v] - ez[z][v]))
            hz[z][v] = hz[z][v] - ((ey_x[z][v] - ey[z][v]) - (ex_y[v] - ex[z][v]))
        hz_y, hx_y = behind_y(hz[z], m), behind_y(hx[z], m)
        hx_z, hy_z = (hx[z - 1], hy[z - 1]) if z > 0 else (edge, edge)
        for v in range(HALF):
            curl_x = (hz[z][v] - hz_y[v]) - (hy[z][v] - hy_z[v])
            curl_y = (hx[z][v] - hx_z[v]) - (hz[z][v] - hz_x[z][v])
            curl_z = (hy[z][v] - hy_x[z][v]) - (hx[z][v] - hx_y[v])
            new_e.append(
                (
                    ex[z][v] + c[z][v] * curl_x,
                    ey[z][v] + c[z][v] * curl_y,
                    ez[z][v] + c[z][v] * curl_z,
                )
            )
    for z in range(SLAB):
        for v in range(HALF):
            for comp, h in enumerate((hx, hy, hz)):
                h_now[comp, z, v] = h[z][v]
                e_new[comp, z, v] = new_e[z * HALF + v][comp]
                if keep is not None:
                    keep[comp, z, v] = new_e[z * HALF + v][comp]


def sweep(blocks, planes, one):
    def block(i, _):
        for plane in planes(i):
            one(plane)
        return 0

    lax.fori_loop(0, blocks, block, 0)


def strided(z, v):
    return pl.ds(4 * v + z, 8, stride=8)


def load_rows(src, dst, dst_base, scale):
    def one(x, _):
        for comp in range(3):
            for z in range(SLAB):
                for v in range(HALF):
                    val = src[comp, x, strided(z, v), :]
                    dst[comp, dst_base + x, z, v] = val if scale == 1.0 else val * scale
        return 0

    lax.fori_loop(0, WIDTH, one, 0)


def free_kernel(table, mat, des, dens, e_in, h_in, coef, mask, to_left, to_right, e, h):
    m = masks()
    row = lax.broadcasted_iota(jnp.int32, (8, 16), 0)
    col = lax.broadcasted_iota(jnp.int32, (8, 16), 1)
    dims = (((1,), (1,)), ((), ()))

    def by_sublane(ref, v):
        pick = (col == HALF * row + v).astype(jnp.float32)
        values = ref[...].astype(jnp.float32)
        return lax.dot_general(pick, values, dims, preferred_element_type=jnp.float32)

    for v in range(HALF):
        kind = by_sublane(mat, v)
        flag = by_sublane(des, v)
        base = jnp.zeros(kind.shape, jnp.float32)
        for which in range(table.shape[0]):
            base = base + jnp.where(kind == which, table[which], 0.0)
        for x in range(WIDTH):
            for z in range(SLAB):
                at = x * SLAB + z
                b = jnp.broadcast_to(base[:, at : at + 1], (8, 128))
                d = jnp.broadcast_to(flag[:, at : at + 1], (8, 128))
                eps = b + d * dens[x, strided(z, v), :]
                coef[x, z, v] = (COEF_E * COEF_H) / eps
                mask[x, z, v] = d * (1.0 / STEPS)
    to_left[2 * STEPS :] = coef[:DEPTH]
    to_right[2 * STEPS :] = coef[WIDTH - DEPTH :]

    load_rows(e_in, e, 0, 1.0)
    load_rows(h_in, h, 1, 1.0 / COEF_H)
    e[:, WIDTH] = jnp.zeros((3,) + CELLS, jnp.float32)
    h[:, 0] = jnp.zeros((3,) + CELLS, jnp.float32)
    to_left[0:2] = e[1:3, 0]

    def one(x):
        update_plane(e.at[:, x], e.at[:, x + 1], h.at[:, x + 1], h.at[:, x], coef.at[x], e.at[:, x], m)

    def early(s, _):
        sweep(WIDTH // 4, lambda i: [4 * i + k for k in range(4)], one)
        to_left[pl.ds(2 * s, 2)] = e[1:3, 0]
        to_right[pl.ds(2 * s - 2, 2)] = h[1:3, WIDTH]
        return 0

    def late(s, _):
        blocks = (STEPS + 2 - s) // 2
        high = WIDTH - 2 * blocks
        sweep(blocks, lambda i: [2 * i, high + 2 * i, 2 * i + 1, high + 2 * i + 1], one)

        @pl.when(s < STEPS)
        def _():
            to_left[pl.ds(2 * s, 2)] = e[1:3, 0]

        to_right[pl.ds(2 * s - 2, 2)] = h[1:3, WIDTH]
        return 0

    lax.fori_loop(1, DEPTH + 1, early, 0)
    lax.fori_loop(DEPTH + 1, STEPS + 1, late, 0)


def full_kernel(
    scale, info, e_in, h_in, coef, from_left, from_right, forward, mask, profile,
    e_out, h_out, g0, g1, g2, g3, over,
    e, now, h, el, hl, er, hr, wide, grad,
):
    m = masks()
    load_rows(e_in, now, 0, 1.0)
    load_rows(h_in, h, 1, 1.0 / COEF_H)
    for ref in (el, hl, er, hr):
        ref[...] = jnp.zeros(ref.shape, jnp.float32)
    inner = (info[0] > 0).astype(jnp.float32)

    def left(x):
        update_plane(
            el.at[:, x + 1], el.at[:, x + 2], hl.at[:, x + 1], hl.at[:, x],
            from_left.at[2 * STEPS + x], el.at[:, x + 1], m,
        )

    def right(x):
        update_plane(
            er.at[:, x], er.at[:, x + 1], hr.at[:, x + 1], hr.at[:, x],
            from_right.at[2 * STEPS + x], er.at[:, x], m,
        )

    def halos(s):
        el[1:3, DEPTH + 1] = now[1:3, 0]
        blocks = (jnp.minimum(s + 1, STEPS - s) + 1) // 2
        low = DEPTH - 2 * blocks
        sweep(
            blocks,
            lambda i: [(left, low + 2 * i), (right, 2 * i), (left, low + 2 * i + 1), (right, 2 * i + 1)],
            lambda job: job[0](job[1]),
        )

    def step(s, _):
        now[1:3, WIDTH] = er[1:3, 0] + from_right[pl.ds(2 * s - 2, 2)]
        h[1:3, 0] = hl[1:3, DEPTH] * inner + from_left[pl.ds(2 * s - 2, 2)]

        def own(x):
            update_plane(
                now.at[:, x], now.at[:, x + 1], h.at[:, x + 1], h.at[:, x], coef.at[x], now.at[:, x], m,
                e.at[s - 1, :, x],
            )

        sweep(WIDTH // 4, lambda i: [4 * i + k for k in range(4)], own)
        hr[1:3, 0] = h[1:3, WIDTH]
        halos(s)
        return 0

    halos(0)
    lax.fori_loop(1, STEPS + 1, step, 0)

    port = info[1]
    omegas = [OMEGA * (f + 1) for f in range(FREQS)]
    mid = (STEPS + 1) / 2
    ca = [float(np.cos(w * mid)) for w in omegas]
    sa = [float(np.sin(w * mid)) for w in omegas]

    def finish(x, acc):
        for f in range(FREQS):
            for q in range(2):
                for comp in range(3):
                    wide[(f * 2 + q) * 3 + comp] = forward[f, q, comp, x].astype(jnp.float32)

        def at_z(z, acc):
            acc = list(acc)
            for v in range(HALF):
                total = None
                for comp in range(3):
                    plus, minus = [], []
                    for i in range(STEPS // 2):
                        lo = e[STEPS // 2 - 1 - i, comp, x, z, v]
                        hi = e[STEPS // 2 + i, comp, x, z, v]
                        plus.append(hi + lo)
                        minus.append(hi - lo)
                    for f in range(FREQS):
                        even = odd = None
                        for i in range(STEPS // 2):
                            c = float(np.cos(omegas[f] * (i + 0.5)))
                            s = float(np.sin(omegas[f] * (i + 0.5)))
                            even = c * plus[i] if even is None else even + c * plus[i]
                            odd = s * minus[i] if odd is None else odd + s * minus[i]
                        if comp == 1:
                            acc[(f * 2) * HALF + v] += even
                            acc[(f * 2 + 1) * HALF + v] += odd
                        re = wide[(f * 2) * 3 + comp, strided(z, v), :]
                        im = wide[(f * 2 + 1) * 3 + comp, strided(z, v), :]
                        term = even * (re * ca[f] + im * sa[f]) + odd * (im * ca[f] - re * sa[f])
                        total = term if total is None else total + term
                grad[lax.rem(z - port + SLAB, SLAB), x, v] = mask[x, z, v] * total
            return tuple(acc)

        acc = lax.fori_loop(0, SLAB, at_z, acc)

        def put(z, _):
            for v in range(HALF):
                for comp in range(3):
                    e_out[comp, x, strided(z, v), :] = now[comp, x, z, v]
                    h_out[comp, x, strided(z, v), :] = h[comp, x + 1, z, v] * COEF_H
            return 0

        lax.fori_loop(0, SLAB, put, 0)
        return acc

    zero = jnp.zeros((8, 128), jnp.float32)
    acc = lax.fori_loop(0, WIDTH, finish, (zero,) * (FREQS * 2 * HALF))
    for f in range(FREQS):
        even = sum(acc[(f * 2) * HALF + v] * profile[info[2], v] for v in range(HALF))
        odd = sum(acc[(f * 2 + 1) * HALF + v] * profile[info[2], v] for v in range(HALF))
        re = ca[f] * even - sa[f] * odd
        im = -(sa[f] * even + ca[f] * odd)
        for q, val in enumerate((re, im)):
            val = jnp.sum(jnp.sum(val, axis=0, keepdims=True), axis=1, keepdims=True)
            over[2 * f + q : 2 * f + q + 1, :] = jnp.broadcast_to(val * scale, (1, 128))
    for d, ref in enumerate((g0, g1, g2, g3)):
        ref[...] = grad[d]


def sum_kernel(a, b, c, d, out):
    for x in range(WIDTH):
        for v in range(HALF):
            out[x, pl.ds(v, 8, stride=2), :] = (a[x, v] + b[x, v]) + (c[x, v] + d[x, v])


def f32(*shape):
    return jax.ShapeDtypeStruct(shape, jnp.float32)


VMEM = pl.BlockSpec(memory_space=pltpu.VMEM)
SMEM = pl.BlockSpec(memory_space=pltpu.SMEM)
PARAMS = pltpu.CompilerParams(vmem_limit_bytes=58 * 1024 * 1024)


def body(e_start, h_start, forward, density, material, design, eps_table, profiles, port_mode):
    tiles = lax.axis_size("tile")
    ports = lax.axis_size("port")
    tile = lax.axis_index("tile")
    port = lax.axis_index("port")

    e_rows, h_rows = rows(e_start[0]), rows(h_start[0])
    sent = f32(2 * STEPS + DEPTH, *CELLS)
    coef, mask, to_left, to_right = pl.pallas_call(
        free_kernel,
        out_shape=(f32(WIDTH, *CELLS), f32(WIDTH, *CELLS), sent, sent),
        in_specs=[SMEM] + [VMEM] * 5,
        out_specs=(VMEM,) * 4,
        scratch_shapes=[pltpu.VMEM((3, WIDTH + 1) + CELLS, jnp.float32)] * 2,
        compiler_params=PARAMS,
        name="free",
    )(eps_table, material.reshape(64, 16), design.reshape(64, 16), rows(density), e_rows, h_rows)
    from_right = lax.ppermute(to_left, "tile", [(i + 1, i) for i in range(tiles - 1)])
    from_left = lax.ppermute(to_right, "tile", [(i, i + 1) for i in range(tiles - 1)])

    info = jnp.stack([tile.astype(jnp.int32), port.astype(jnp.int32), port_mode[0]])
    profile = profiles.reshape(-1, 8, HALF, 128).transpose(0, 2, 1, 3)
    scale = 1.0 / math.sqrt(WIDTH * tiles * SLAB * 2048)
    e_out, h_out, *parts, over = pl.pallas_call(
        functools.partial(full_kernel, scale),
        out_shape=(f32(3, WIDTH, 64, 128), f32(3, WIDTH, 64, 128))
        + (f32(WIDTH, HALF, 8, 128),) * SLAB
        + (f32(2 * FREQS, 128),),
        in_specs=[SMEM] + [VMEM] * 8,
        out_specs=(VMEM,) * (3 + SLAB),
        scratch_shapes=[
            pltpu.VMEM((STEPS, 3, WIDTH) + CELLS, jnp.float32),
            pltpu.VMEM((3, WIDTH + 1) + CELLS, jnp.float32),
            pltpu.VMEM((3, WIDTH + 1) + CELLS, jnp.float32),
            pltpu.VMEM((3, DEPTH + 2) + CELLS, jnp.float32),
            pltpu.VMEM((3, DEPTH + 1) + CELLS, jnp.float32),
            pltpu.VMEM((3, DEPTH + 1) + CELLS, jnp.float32),
            pltpu.VMEM((3, DEPTH + 1) + CELLS, jnp.float32),
            pltpu.VMEM((4 * 3, 64, 128), jnp.float32),
            pltpu.VMEM((SLAB, WIDTH, HALF, 8, 128), jnp.float32),
        ],
        compiler_params=PARAMS,
        name="full",
    )(info, e_rows, h_rows, coef, from_left, from_right, rows(forward[0]), mask, profile)

    for d in range(1, ports):
        parts[d] = lax.ppermute(parts[d], "port", [(i, (i + d) % ports) for i in range(ports)])
    total = over
    span = 1
    while span < tiles:
        radix = min(4, tiles // span)
        if span * radix >= tiles:
            total, *parts = lax.optimization_barrier((total, *parts))
        got = []
        for d in range(1, radix):
            pairs = []
            for i in range(tiles):
                digit = i // span % radix
                pairs.append((i, i + ((digit + d) % radix - digit) * span))
            got.append(lax.ppermute(total, "tile", pairs))
        total = total + sum(got[1:], got[0])
        span *= radix
    gradient = pl.pallas_call(
        sum_kernel,
        out_shape=f32(WIDTH, 16, 128),
        in_specs=[VMEM] * 4,
        out_specs=VMEM,
        name="total",
    )(*parts)
    return (
        unrows(e_out)[None],
        unrows(h_out)[None],
        gradient.reshape(WIDTH, 1, 2048),
        total[:, 0].reshape(1, FREQS, 2),
    )


def solution(mesh):
    return jax.shard_map(
        body,
        mesh=mesh,
        in_specs=(
            P("port", None, "tile", None, None),
            P("port", None, "tile", None, None),
            P("port", None, None, None, "tile", None, None),
            P("tile", None, None),
            P("tile", None, None),
            P("tile", None, None),
            P(),
            P(),
            P("port"),
        ),
        out_specs=(
            P("port", None, "tile", None, None),
            P("port", None, "tile", None, None),
            P("tile", "port", None),
            P("port", None, None),
        ),
        check_vma=False,
    )
```

```python
import functools
import math

import jax
import jax.numpy as jnp
import numpy as np
from jax import lax
from jax.experimental import pallas as pl
from jax.experimental.pallas import tpu as pltpu
from jax.sharding import PartitionSpec as P

STEPS = 16
OMEGA = 0.7
COEF_H = 0.5
COEF_E = 0.5

WIDTH = 16
SLAB = 4
HALF = 2
DEPTH = STEPS // 2
FREQS = 2
CELLS = (SLAB, HALF, 8, 128)


def rows(x):
    lead = x.shape[:-2]
    x = x.reshape(lead + (SLAB, 16, 128))
    return jnp.swapaxes(x, -3, -2).reshape(lead + (64, 128))


def unrows(x):
    lead = x.shape[:-2]
    x = x.reshape(lead + (16, SLAB, 128))
    return jnp.swapaxes(x, -3, -2).reshape(lead + (SLAB, 2048))


def masks():
    lane = lax.broadcasted_iota(jnp.int32, (8, 128), 1)
    sub = lax.broadcasted_iota(jnp.int32, (8, 128), 0)
    return lane == 127, lane == 0, sub == 7, sub == 0


def ahead_y(pair, m):
    r0 = pltpu.roll(pair[0], 127, 1)
    r1 = pltpu.roll(pair[1], 127, 1)
    rs = jnp.where(m[2], 0.0, pltpu.roll(r0, 7, 0))
    return jnp.where(m[0], r1, r0), jnp.where(m[0], rs, r1)


def behind_y(pair, m):
    r0 = pltpu.roll(pair[0], 1, 1)
    r1 = pltpu.roll(pair[1], 1, 1)
    rs = jnp.where(m[3], 0.0, pltpu.roll(r1, 1, 0))
    return jnp.where(m[1], rs, r0), jnp.where(m[1], r0, r1)


def update_plane(e_old, e_next, h_now, h_prev, coef, e_new, m, keep=None, sums=None):
    def plane(ref, comp):
        return [[ref[comp, z, v] for v in range(HALF)] for z in range(SLAB)]

    ex, ey, ez = (plane(e_old, comp) for comp in range(3))
    ey_x, ez_x = plane(e_next, 1), plane(e_next, 2)
    hx, hy, hz = (plane(h_now, comp) for comp in range(3))
    hy_x, hz_x = plane(h_prev, 1), plane(h_prev, 2)
    c = [[coef[z, v] for v in range(HALF)] for z in range(SLAB)]
    edge = [0.0] * HALF
    new_e = []
    for z in range(SLAB):
        ex_z, ey_z = (ex[z + 1], ey[z + 1]) if z + 1 < SLAB else (edge, edge)
        ez_y, ex_y = ahead_y(ez[z], m), ahead_y(ex[z], m)
        for v in range(HALF):
            hx[z][v] = hx[z][v] - ((ez_y[v] - ez[z][v]) - (ey_z[v] - ey[z][v]))
            hy[z][v] = hy[z][v] - ((ex_z[v] - ex[z][v]) - (ez_x[z][v] - ez[z][v]))
            hz[z][v] = hz[z][v] - ((ey_x[z][v] - ey[z][v]) - (ex_y[v] - ex[z][v]))
        hz_y, hx_y = behind_y(hz[z], m), behind_y(hx[z], m)
        hx_z, hy_z = (hx[z - 1], hy[z - 1]) if z > 0 else (edge, edge)
        for v in range(HALF):
            curl_x = (hz[z][v] - hz_y[v]) - (hy[z][v] - hy_z[v])
            curl_y = (hx[z][v] - hx_z[v]) - (hz[z][v] - hz_x[z][v])
            curl_z = (hy[z][v] - hy_x[z][v]) - (hx[z][v] - hx_y[v])
            new_e.append(
                (
                    ex[z][v] + c[z][v] * curl_x,
                    ey[z][v] + c[z][v] * curl_y,
                    ez[z][v] + c[z][v] * curl_z,
                )
            )
    for z in range(SLAB):
        for v in range(HALF):
            for comp, h in enumerate((hx, hy, hz)):
                h_now[comp, z, v] = h[z][v]
                e_new[comp, z, v] = new_e[z * HALF + v][comp]
                if keep is not None:
                    keep[comp, z, v] = new_e[z * HALF + v][comp]
    if sums is not None:
        for v in range(HALF):
            sums[v] += sum(new_e[z * HALF + v][1] for z in range(SLAB))


def sweep(blocks, planes, one):
    def block(i, _):
        for plane in planes(i):
            one(plane)
        return 0

    lax.fori_loop(0, blocks, block, 0)


def strided(z, v):
    return pl.ds(4 * v + z, 8, stride=8)


def load_rows(src, dst, scale, first=0, count=WIDTH, base=0):
    def one(x, _):
        for comp in range(3):
            for z in range(SLAB):
                for v in range(HALF):
                    val = src[comp, first + x, strided(z, v), :]
                    dst[comp, base + x, z, v] = val if scale == 1.0 else val * scale
        return 0

    lax.fori_loop(0, count, one, 0)


def by_sublane(ref, v):
    row = lax.broadcasted_iota(jnp.int32, (8, 16), 0)
    col = lax.broadcasted_iota(jnp.int32, (8, 16), 1)
    pick = (col == HALF * row + v).astype(jnp.float32)
    values = ref[...].astype(jnp.float32)
    return lax.dot_general(pick, values, (((1,), (1,)), ((), ())), preferred_element_type=jnp.float32)


def free_kernel(
    info, table, mat_far, des_far, dens_far, e_far, h_far,
    coef_far, inter_far, intra_far,
    ea, ha, eb, hb, coef, mat, des, dens, e_in, h_in, faces, sems, sent,
):
    m = masks()
    to_left, to_right = faces.at[0], faces.at[1]
    odd = lax.rem(info[0], 2)
    pairs = ((mat_far, mat), (des_far, des), (dens_far, dens), (e_far, e_in), (h_far, h_in))
    fetch = [pltpu.make_async_copy(src, dst, sems.at[i]) for i, (src, dst) in enumerate(pairs)]
    for copy in fetch:
        copy.start()
    for copy in fetch[:3]:
        copy.wait()
    for v in range(HALF):
        kind = by_sublane(mat, v)
        flag = by_sublane(des, v)
        base = jnp.zeros(kind.shape, jnp.float32)
        for which in range(table.shape[0]):
            base = base + jnp.where(kind == which, table[which], 0.0)
        for x in range(WIDTH):
            for z in range(SLAB):
                at = x * SLAB + z
                b = jnp.broadcast_to(base[:, at : at + 1], (8, 128))
                d = jnp.broadcast_to(flag[:, at : at + 1], (8, 128))
                eps = b + d * dens[x, strided(z, v), :]
                coef[x, z, v] = (COEF_E * COEF_H) / eps
    coef_out = pltpu.make_async_copy(coef, coef_far, sent.at[4])
    coef_out.start()
    to_left[2 * STEPS :] = coef[:DEPTH]
    to_right[2 * STEPS :] = coef[WIDTH - DEPTH :]

    half = WIDTH // 2
    fetch[3].wait()
    fetch[4].wait()
    load_rows(e_in, ea, 1.0, 0, half)
    load_rows(e_in, eb, 1.0, half, half)
    load_rows(h_in, ha, 1.0 / COEF_H, 0, half, 1)
    load_rows(h_in, hb, 1.0 / COEF_H, half, half, 1)
    eb[:, half] = jnp.zeros((3,) + CELLS, jnp.float32)
    ha[:, 0] = jnp.zeros((3,) + CELLS, jnp.float32)
    to_left[0:2] = ea[1:3, 0]

    def low(x):
        update_plane(ea.at[:, x], ea.at[:, x + 1], ha.at[:, x + 1], ha.at[:, x], coef.at[x], ea.at[:, x], m)

    def high(x):
        update_plane(eb.at[:, x], eb.at[:, x + 1], hb.at[:, x + 1], hb.at[:, x], coef.at[half + x], eb.at[:, x], m)

    def early(s, _):
        ea[1:3, half] = eb[1:3, 0]
        sweep(half // 4, lambda i: [4 * i + k for k in range(4)], low)
        hb[1:3, 0] = ha[1:3, half]
        sweep(half // 4, lambda i: [4 * i + k for k in range(4)], high)
        to_left[pl.ds(2 * s, 2)] = ea[1:3, 0]
        to_right[pl.ds(2 * s - 2, 2)] = hb[1:3, half]
        return 0

    def late(s, _):
        blocks = (STEPS + 2 - s) // 2
        first = half - 2 * blocks
        sweep(
            blocks,
            lambda i: [(low, 2 * i), (high, first + 2 * i), (low, 2 * i + 1), (high, first + 2 * i + 1)],
            lambda job: job[0](job[1]),
        )

        @pl.when(s < STEPS)
        def _():
            to_left[pl.ds(2 * s, 2)] = ea[1:3, 0]

        to_right[pl.ds(2 * s - 2, 2)] = hb[1:3, half]
        return 0

    lax.fori_loop(1, DEPTH + 1, early, 0)
    cut = 2 * DEPTH
    sends = []
    for first, count in ((0, cut), (cut, 2 * STEPS + DEPTH - cut)):
        for side, far in ((odd, inter_far), (1 - odd, intra_far)):
            part = pl.ds(first, count)
            sends.append(pltpu.make_async_copy(faces.at[side, part], far.at[part], sent.at[len(sends)]))
    sends[0].start()
    sends[1].start()
    lax.fori_loop(DEPTH + 1, STEPS + 1, late, 0)
    sends[2].start()
    sends[3].start()
    for copy in sends + [coef_out]:
        copy.wait()


def angles():
    omegas = [OMEGA * (f + 1) for f in range(FREQS)]
    mid = (STEPS + 1) / 2
    return omegas, [float(np.cos(w * mid)) for w in omegas], [float(np.sin(w * mid)) for w in omegas]


def wide_kernel(forward, des, profile_in, e_in, h_in, turned, profile, e_all, h_all, wide, mask):
    _, ca, sa = angles()
    profile[...] = profile_in[...]
    for v in range(HALF):
        flag = by_sublane(des, v)
        for x in range(WIDTH):
            for z in range(SLAB):
                at = x * SLAB + z
                mask[x, z, v] = jnp.broadcast_to(flag[:, at : at + 1], (8, 128)) * (1.0 / STEPS)
    load_rows(e_in, e_all, 1.0)
    load_rows(h_in, h_all, 1.0 / COEF_H)

    def one(x, _):
        for f in range(FREQS):
            for q in range(2):
                for comp in range(3):
                    wide[(f * 2 + q) * 3 + comp] = forward[f, q, comp, x].astype(jnp.float32)

        def at_z(z, _):
            for v in range(HALF):
                keep = mask[x, z, v]
                for f in range(FREQS):
                    for comp in range(3):
                        re = wide[(f * 2) * 3 + comp, strided(z, v), :]
                        im = wide[(f * 2 + 1) * 3 + comp, strided(z, v), :]
                        turned[f, 0, comp, z, x, v] = keep * (re * ca[f] + im * sa[f])
                        turned[f, 1, comp, z, x, v] = keep * (im * ca[f] - re * sa[f])
            return 0

        return lax.fori_loop(0, SLAB, at_z, 0)

    lax.fori_loop(0, WIDTH, one, 0)


def terms(away, info, e, turned, grad):
    omegas, _, _ = angles()
    z = lax.rem(info[1] + away, SLAB)

    def one(x, _):
        for v in range(HALF):
            total = None
            for comp in range(3):
                plus, minus = [], []
                for i in range(STEPS // 2):
                    lo = e[STEPS // 2 - 1 - i, comp, x, z, v]
                    hi = e[STEPS // 2 + i, comp, x, z, v]
                    plus.append(hi + lo)
                    minus.append(hi - lo)
                for f in range(FREQS):
                    even = odd = None
                    for i in range(STEPS // 2):
                        c = float(np.cos(omegas[f] * (i + 0.5)))
                        s = float(np.sin(omegas[f] * (i + 0.5)))
                        even = c * plus[i] if even is None else even + c * plus[i]
                        odd = s * minus[i] if odd is None else odd + s * minus[i]
                    term = even * turned[f, 0, comp, z, x, v] + odd * turned[f, 1, comp, z, x, v]
                    total = term if total is None else total + term
            grad[x, v] = total
        return 0

    lax.fori_loop(0, WIDTH, one, 0)


def out_kernel(e, h, e_out, h_out):
    def one(x, _):
        for z in range(SLAB):
            for v in range(HALF):
                for comp in range(3):
                    e_out[comp, x, strided(z, v), :] = e[comp, x, z, v]
                    h_out[comp, x, strided(z, v), :] = h[comp, x + 1, z, v] * COEF_H
        return 0

    lax.fori_loop(0, WIDTH, one, 0)


def steps_kernel(
    scale, info, e_all, h_all, coef, inter, intra, profile, turned,
    now, h, over, *rest,
):
    grads_far, (e, el, hl, er, hr, sums, *grads, got, sems) = rest[:SLAB], rest[SLAB:]
    m = masks()
    odd = lax.rem(info[0], 2)
    fetch = [
        pltpu.make_async_copy(far, got.at[side], sems.at[SLAB + i])
        for i, (side, far) in enumerate(((odd, inter), (1 - odd, intra)))
    ]
    for copy in fetch:
        copy.start()
    from_left, from_right = got.at[0], got.at[1]

    def place(x, _):
        for comp in range(3):
            now[comp, x] = e_all[comp, x]
            h[comp, x + 1] = h_all[comp, x]
        return 0

    lax.fori_loop(0, WIDTH, place, 0)
    sums[...] = jnp.zeros(sums.shape, jnp.float32)
    for ref in (el, hl, er, hr):
        ref[...] = jnp.zeros(ref.shape, jnp.float32)
    inner = (info[0] > 0).astype(jnp.float32)

    def left(x):
        update_plane(
            el.at[:, x + 1], el.at[:, x + 2], hl.at[:, x + 1], hl.at[:, x],
            from_left.at[2 * STEPS + x], el.at[:, x + 1], m,
        )

    def right(x):
        update_plane(
            er.at[:, x], er.at[:, x + 1], hr.at[:, x + 1], hr.at[:, x],
            from_right.at[2 * STEPS + x], er.at[:, x], m,
        )

    def halos(s):
        el[1:3, DEPTH + 1] = now[1:3, 0]
        blocks = (jnp.minimum(s + 1, STEPS - s) + 1) // 2
        low = DEPTH - 2 * blocks
        sweep(
            blocks,
            lambda i: [(left, low + 2 * i), (right, 2 * i), (left, low + 2 * i + 1), (right, 2 * i + 1)],
            lambda job: job[0](job[1]),
        )

    def step(s, _):
        now[1:3, WIDTH] = er[1:3, 0] + from_right[pl.ds(2 * s - 2, 2)]
        h[1:3, 0] = hl[1:3, DEPTH] * inner + from_left[pl.ds(2 * s - 2, 2)]

        def own(x):
            update_plane(
                now.at[:, x], now.at[:, x + 1], h.at[:, x + 1], h.at[:, x], coef.at[x], now.at[:, x], m,
                e.at[s - 1, :, x], sums.at[s - 1],
            )

        sweep(WIDTH // 4, lambda i: [4 * i + k for k in range(4)], own)
        hr[1:3, 0] = h[1:3, WIDTH]
        halos(s)
        return 0

    for copy in fetch:
        copy.wait()
    halos(0)
    lax.fori_loop(1, STEPS + 1, step, 0)

    omegas = [OMEGA * (f + 1) for f in range(FREQS)]
    profiled = [sum(sums[t, v] * profile[strided(info[2], v), :] for v in range(HALF)) for t in range(STEPS)]
    for f in range(FREQS):
        for q in range(2):
            turn = [float(np.cos(omegas[f] * (t + 1))) if q == 0 else -float(np.sin(omegas[f] * (t + 1))) for t in range(STEPS)]
            val = sum(turn[t] * profiled[t] for t in range(STEPS))
            val = jnp.sum(jnp.sum(val, axis=0, keepdims=True), axis=1, keepdims=True)
            over[2 * f + q : 2 * f + q + 1, :] = jnp.broadcast_to(val * scale, (1, 128))
    copies = []
    for away in (1, 2, 3, 0):
        terms(away, info, e, turned, grads[away])
        copies.append(pltpu.make_async_copy(grads[away], grads_far[away], sems.at[away]))
        copies[-1].start()
    for copy in copies:
        copy.wait()


def sum_kernel(a, b, c, d, out):
    for x in range(WIDTH):
        for v in range(HALF):
            out[x, pl.ds(v, 8, stride=2), :] = (a[x, v] + b[x, v]) + (c[x, v] + d[x, v])


def add_kernel(*refs):
    total = refs[0][...]
    for ref in refs[1:-1]:
        total = total + ref[...]
    refs[-1][...] = total


def f32(*shape):
    return jax.ShapeDtypeStruct(shape, jnp.float32)


VMEM = pl.BlockSpec(memory_space=pltpu.VMEM)
SMEM = pl.BlockSpec(memory_space=pltpu.SMEM)
FAR = pl.BlockSpec(memory_space=pltpu.HBM)
ANY = pl.BlockSpec(memory_space=pl.ANY)


def room(mib):
    return pltpu.CompilerParams(vmem_limit_bytes=mib * 1024 * 1024)


def held(*shape):
    return pltpu.VMEM(shape, jnp.float32)


def here(x):
    return pltpu.with_memory_space_constraint(x, pltpu.VMEM)


def far(x):
    return pltpu.with_memory_space_constraint(x, pltpu.HBM)


def body(e_start, h_start, forward, density, material, design, eps_table, profiles, port_mode):
    tiles = lax.axis_size("tile")
    ports = lax.axis_size("port")
    tile = lax.axis_index("tile")
    port = lax.axis_index("port")

    e_rows, h_rows = rows(e_start[0]), rows(h_start[0])
    planes = 2 * STEPS + DEPTH
    sent = pltpu.HBM((planes, *CELLS), jnp.float32)
    half = (3, WIDTH // 2 + 1) + CELLS
    info = jnp.stack([tile.astype(jnp.int32), port.astype(jnp.int32), port_mode[0]])
    coef, inter, intra = pl.pallas_call(
        free_kernel,
        out_shape=(pltpu.HBM((WIDTH, *CELLS), jnp.float32), sent, sent),
        in_specs=[SMEM] * 2 + [FAR] * 5,
        out_specs=(FAR,) * 3,
        scratch_shapes=[held(*half)] * 4
        + [
            held(WIDTH, *CELLS),
            pltpu.VMEM((64, 16), jnp.int32),
            pltpu.VMEM((64, 16), jnp.int32),
            held(WIDTH, 64, 128),
            held(3, WIDTH, 64, 128),
            held(3, WIDTH, 64, 128),
            held(2, planes, *CELLS),
            pltpu.SemaphoreType.DMA((5,)),
            pltpu.SemaphoreType.DMA((5,)),
        ],
        compiler_params=room(14),
        name="free",
    )(
        info, eps_table, far(material.reshape(64, 16)), far(design.reshape(64, 16)), far(rows(density)),
        far(e_rows), far(h_rows),
    )
    across = [(i, i + 1) for i in range(1, tiles - 1, 2)]
    inter = lax.ppermute(inter, "tile", across + [(j, i) for i, j in across])
    intra = lax.ppermute(intra, "tile", [(i, i ^ 1) for i in range(tiles)])

    fields = held(3, WIDTH, *CELLS)
    turned, profile, e_all, h_all = pl.pallas_call(
        wide_kernel,
        out_shape=(held(FREQS, 2, 3, SLAB, WIDTH, HALF, 8, 128), f32(64, 128), fields, fields),
        in_specs=[VMEM] * 5,
        out_specs=(VMEM,) * 4,
        scratch_shapes=[held(4 * 3, 64, 128), held(WIDTH, *CELLS)],
        compiler_params=room(4),
        name="wide",
    )(rows(forward[0]), design.reshape(64, 16), rows(profiles), e_rows, h_rows)

    scale = 1.0 / math.sqrt(WIDTH * tiles * SLAB * 2048)
    edge = (3, DEPTH + 1) + CELLS
    wider = held(3, WIDTH + 1, *CELLS)
    e_last, h_last, over, *parts = pl.pallas_call(
        functools.partial(steps_kernel, scale),
        out_shape=(wider, wider, f32(2 * FREQS, 128)) + (pltpu.HBM((WIDTH, HALF, 8, 128), jnp.float32),) * SLAB,
        in_specs=[SMEM] + [VMEM] * 3 + [ANY] * 2 + [VMEM] * 2,
        out_specs=(VMEM,) * 3 + (FAR,) * SLAB,
        scratch_shapes=[
            held(STEPS, 3, WIDTH, *CELLS),
            held(3, DEPTH + 2, *CELLS),
            held(*edge),
            held(*edge),
            held(*edge),
            held(STEPS, HALF, 8, 128),
        ]
        + [held(WIDTH, HALF, 8, 128)] * SLAB
        + [held(2, planes, *CELLS), pltpu.SemaphoreType.DMA((SLAB + 2,))],
        compiler_params=room(39),
        name="steps",
    )(info, here(e_all), here(h_all), coef, inter, intra, profile, here(turned))

    def to_port(x, d):
        return lax.ppermute(x, "port", [(i, (i + d) % ports) for i in range(ports)])

    def stage(total, steps):
        got = []
        for mask in range(1, 1 << len(steps)):
            flip = sum(by for bit, by in enumerate(steps) if mask >> bit & 1)
            got.append(lax.ppermute(total, "tile", [(i, i ^ flip) for i in range(tiles)]))
        return pl.pallas_call(
            add_kernel,
            out_shape=f32(*total.shape),
            in_specs=[VMEM] * (1 + len(got)),
            out_specs=VMEM,
            compiler_params=room(1),
            name="add",
        )(total, *got)

    e_out, h_out = pl.pallas_call(
        out_kernel,
        out_shape=(f32(3, WIDTH, 64, 128), f32(3, WIDTH, 64, 128)),
        in_specs=[VMEM] * 2,
        out_specs=(VMEM,) * 2,
        compiler_params=room(4),
        name="out",
    )(here(e_last), here(h_last))
    total = stage(over, (1, 8))
    total, e_out, h_out, *parts = lax.optimization_barrier((total, e_out, h_out, *parts))
    for d in range(1, ports):
        parts[d] = to_port(parts[d], d)
    total = stage(total, (2, 4))
    total, *parts = lax.optimization_barrier((total, *parts))
    total = stage(total, (16, 32))
    gradient = pl.pallas_call(
        sum_kernel,
        out_shape=f32(WIDTH, 16, 128),
        in_specs=[VMEM] * 4,
        out_specs=VMEM,
        name="total",
    )(*parts)
    return (
        unrows(e_out)[None],
        unrows(h_out)[None],
        gradient.reshape(WIDTH, 1, 2048),
        total[:, 0].reshape(1, FREQS, 2),
    )


def solution(mesh):
    return jax.shard_map(
        body,
        mesh=mesh,
        in_specs=(
            P("port", None, "tile", None, None),
            P("port", None, "tile", None, None),
            P("port", None, None, None, "tile", None, None),
            P("tile", None, None),
            P("tile", None, None),
            P("tile", None, None),
            P(),
            P(),
            P("port"),
        ),
        out_specs=(
            P("port", None, "tile", None, None),
            P("port", None, "tile", None, None),
            P("tile", "port", None),
            P("port", None, None),
        ),
        check_vma=False,
    )
```

```python
import functools
import math

import jax
import jax.numpy as jnp
import numpy as np
from jax import lax
from jax.experimental import pallas as pl
from jax.experimental.pallas import tpu as pltpu
from jax.sharding import PartitionSpec as P

STEPS = 16
OMEGA = 0.7
COEF_H = 0.5
COEF_E = 0.5

WIDTH = 16
SLAB = 4
HALF = 2
DEPTH = STEPS // 2
FREQS = 2
CELLS = (SLAB, HALF, 8, 128)


def rows(x):
    lead = x.shape[:-2]
    x = x.reshape(lead + (SLAB, 16, 128))
    return jnp.swapaxes(x, -3, -2).reshape(lead + (64, 128))


def unrows(x):
    lead = x.shape[:-2]
    x = x.reshape(lead + (16, SLAB, 128))
    return jnp.swapaxes(x, -3, -2).reshape(lead + (SLAB, 2048))


def masks():
    lane = lax.broadcasted_iota(jnp.int32, (8, 128), 1)
    sub = lax.broadcasted_iota(jnp.int32, (8, 128), 0)
    return lane == 127, lane == 0, sub == 7, sub == 0


def ahead_y(pair, m):
    r0 = pltpu.roll(pair[0], 127, 1)
    r1 = pltpu.roll(pair[1], 127, 1)
    rs = jnp.where(m[2], 0.0, pltpu.roll(r0, 7, 0))
    return jnp.where(m[0], r1, r0), jnp.where(m[0], rs, r1)


def behind_y(pair, m):
    r0 = pltpu.roll(pair[0], 1, 1)
    r1 = pltpu.roll(pair[1], 1, 1)
    rs = jnp.where(m[3], 0.0, pltpu.roll(r1, 1, 0))
    return jnp.where(m[1], rs, r0), jnp.where(m[1], r0, r1)


def update_plane(e_old, e_next, h_now, h_prev, coef, e_new, m, keep=None, sums=None):
    def plane(ref, comp):
        return [[ref[comp, z, v] for v in range(HALF)] for z in range(SLAB)]

    ex, ey, ez = (plane(e_old, comp) for comp in range(3))
    ey_x, ez_x = plane(e_next, 1), plane(e_next, 2)
    hx, hy, hz = (plane(h_now, comp) for comp in range(3))
    hy_x, hz_x = plane(h_prev, 1), plane(h_prev, 2)
    c = [[coef[z, v] for v in range(HALF)] for z in range(SLAB)]
    edge = [0.0] * HALF
    new_e = []
    for z in range(SLAB):
        ex_z, ey_z = (ex[z + 1], ey[z + 1]) if z + 1 < SLAB else (edge, edge)
        ez_y, ex_y = ahead_y(ez[z], m), ahead_y(ex[z], m)
        for v in range(HALF):
            hx[z][v] = hx[z][v] - ((ez_y[v] - ez[z][v]) - (ey_z[v] - ey[z][v]))
            hy[z][v] = hy[z][v] - ((ex_z[v] - ex[z][v]) - (ez_x[z][v] - ez[z][v]))
            hz[z][v] = hz[z][v] - ((ey_x[z][v] - ey[z][v]) - (ex_y[v] - ex[z][v]))
        hz_y, hx_y = behind_y(hz[z], m), behind_y(hx[z], m)
        hx_z, hy_z = (hx[z - 1], hy[z - 1]) if z > 0 else (edge, edge)
        for v in range(HALF):
            curl_x = (hz[z][v] - hz_y[v]) - (hy[z][v] - hy_z[v])
            curl_y = (hx[z][v] - hx_z[v]) - (hz[z][v] - hz_x[z][v])
            curl_z = (hy[z][v] - hy_x[z][v]) - (hx[z][v] - hx_y[v])
            new_e.append(
                (
                    ex[z][v] + c[z][v] * curl_x,
                    ey[z][v] + c[z][v] * curl_y,
                    ez[z][v] + c[z][v] * curl_z,
                )
            )
    for z in range(SLAB):
        for v in range(HALF):
            for comp, h in enumerate((hx, hy, hz)):
                h_now[comp, z, v] = h[z][v]
                e_new[comp, z, v] = new_e[z * HALF + v][comp]
                if keep is not None:
                    keep[comp, z, v] = new_e[z * HALF + v][comp]
    if sums is not None:
        for v in range(HALF):
            sums[v] += sum(new_e[z * HALF + v][1] for z in range(SLAB))


def sweep(blocks, planes, one):
    def block(i, _):
        for plane in planes(i):
            one(plane)
        return 0

    lax.fori_loop(0, blocks, block, 0)


def strided(z, v):
    return pl.ds(4 * v + z, 8, stride=8)


def load_rows(src, dst, scale, first=0, count=WIDTH, base=0):
    def one(x, _):
        for comp in range(3):
            for z in range(SLAB):
                for v in range(HALF):
                    val = src[comp, first + x, strided(z, v), :]
                    dst[comp, base + x, z, v] = val if scale == 1.0 else val * scale
        return 0

    lax.fori_loop(0, count, one, 0)


def by_sublane(ref, v):
    row = lax.broadcasted_iota(jnp.int32, (8, 16), 0)
    col = lax.broadcasted_iota(jnp.int32, (8, 16), 1)
    pick = (col == HALF * row + v).astype(jnp.float32)
    values = ref[...].astype(jnp.float32)
    return lax.dot_general(pick, values, (((1,), (1,)), ((), ())), preferred_element_type=jnp.float32)


def free_planes(ea, ha, eb, hb, coef):
    m = masks()
    half = WIDTH // 2

    def low(x):
        update_plane(ea.at[:, x], ea.at[:, x + 1], ha.at[:, x + 1], ha.at[:, x], coef.at[x], ea.at[:, x], m)

    def high(x):
        update_plane(eb.at[:, x], eb.at[:, x + 1], hb.at[:, x + 1], hb.at[:, x], coef.at[half + x], eb.at[:, x], m)

    return low, high


def swaps(info, faces, inter_far, intra_far, sems):
    odd = lax.rem(info[0], 2)
    return [
        pltpu.make_async_copy(faces.at[side], far, sems.at[i])
        for i, (side, far) in enumerate(((odd, inter_far), (1 - odd, intra_far)))
    ]


def free_kernel(
    info, table, mat_far, des_far, dens_far, e_far, h_far,
    coef, inter_far, intra_far, ea, ha, eb, hb,
    mat, des, dens, e_in, h_in, faces, sems, sent,
):
    to_left, to_right = faces.at[0], faces.at[1]
    pairs = ((mat_far, mat), (des_far, des), (dens_far, dens), (e_far, e_in), (h_far, h_in))
    fetch = [pltpu.make_async_copy(src, dst, sems.at[i]) for i, (src, dst) in enumerate(pairs)]
    for copy in fetch:
        copy.start()
    for copy in fetch[:3]:
        copy.wait()
    for v in range(HALF):
        kind = by_sublane(mat, v)
        flag = by_sublane(des, v)
        base = jnp.zeros(kind.shape, jnp.float32)
        for which in range(table.shape[0]):
            base = base + jnp.where(kind == which, table[which], 0.0)
        for x in range(WIDTH):
            for z in range(SLAB):
                at = x * SLAB + z
                b = jnp.broadcast_to(base[:, at : at + 1], (8, 128))
                d = jnp.broadcast_to(flag[:, at : at + 1], (8, 128))
                eps = b + d * dens[x, strided(z, v), :]
                coef[x, z, v] = (COEF_E * COEF_H) / eps
    to_left[STEPS:] = coef[:DEPTH]
    to_right[STEPS:] = coef[WIDTH - DEPTH :]

    half = WIDTH // 2
    fetch[3].wait()
    fetch[4].wait()
    load_rows(e_in, ea, 1.0, 0, half)
    load_rows(e_in, eb, 1.0, half, half)
    load_rows(h_in, ha, 1.0 / COEF_H, 0, half, 1)
    load_rows(h_in, hb, 1.0 / COEF_H, half, half, 1)
    eb[:, half] = jnp.zeros((3,) + CELLS, jnp.float32)
    ha[:, 0] = jnp.zeros((3,) + CELLS, jnp.float32)
    low, high = free_planes(ea, ha, eb, hb, coef)

    def early(s, _):
        to_left[pl.ds(2 * s - 2, 2)] = ea[1:3, 0]
        ea[1:3, half] = eb[1:3, 0]
        sweep(half // 4, lambda i: [4 * i + k for k in range(4)], low)
        hb[1:3, 0] = ha[1:3, half]
        sweep(half // 4, lambda i: [4 * i + k for k in range(4)], high)
        to_right[pl.ds(2 * s - 2, 2)] = hb[1:3, half]
        return 0

    lax.fori_loop(1, DEPTH + 1, early, 0)
    sends = swaps(info, faces, inter_far, intra_far, sent)
    for copy in sends:
        copy.start()
    for copy in sends:
        copy.wait()


def late_kernel(
    info, coef, ea_in, ha_in, eb_in, hb_in,
    inter_far, intra_far,
    ea, ha, eb, hb, faces, sent,
):
    to_left, to_right = faces.at[0], faces.at[1]
    half = WIDTH // 2

    def place(x, _):
        for comp in range(3):
            for src, dst in ((ea_in, ea), (ha_in, ha), (eb_in, eb), (hb_in, hb)):
                dst[comp, x] = src[comp, x]
        return 0

    lax.fori_loop(0, half + 1, place, 0)
    low, high = free_planes(ea, ha, eb, hb, coef)

    def late(s, _):
        to_left[pl.ds(2 * (s - DEPTH - 1), 2)] = ea[1:3, 0]
        blocks = (STEPS + 2 - s) // 2
        first = half - 2 * blocks
        sweep(
            blocks,
            lambda i: [(low, 2 * i), (high, first + 2 * i), (low, 2 * i + 1), (high, first + 2 * i + 1)],
            lambda job: job[0](job[1]),
        )
        to_right[pl.ds(2 * (s - DEPTH - 1), 2)] = hb[1:3, half]
        return 0

    lax.fori_loop(DEPTH + 1, STEPS + 1, late, 0)
    sends = swaps(info, faces, inter_far, intra_far, sent)
    for copy in sends:
        copy.start()
    for copy in sends:
        copy.wait()


def angles():
    omegas = [OMEGA * (f + 1) for f in range(FREQS)]
    mid = (STEPS + 1) / 2
    return omegas, [float(np.cos(w * mid)) for w in omegas], [float(np.sin(w * mid)) for w in omegas]


def wide_kernel(forward, des, profile_in, e_in, h_in, turned, profile, e_all, h_all, wide, mask):
    _, ca, sa = angles()
    profile[...] = profile_in[...]
    for v in range(HALF):
        flag = by_sublane(des, v)
        for x in range(WIDTH):
            for z in range(SLAB):
                at = x * SLAB + z
                mask[x, z, v] = jnp.broadcast_to(flag[:, at : at + 1], (8, 128)) * (1.0 / STEPS)
    load_rows(e_in, e_all, 1.0)
    load_rows(h_in, h_all, 1.0 / COEF_H)

    def one(x, _):
        for f in range(FREQS):
            for q in range(2):
                for comp in range(3):
                    wide[(f * 2 + q) * 3 + comp] = forward[f, q, comp, x].astype(jnp.float32)

        def at_z(z, _):
            for v in range(HALF):
                keep = mask[x, z, v]
                for f in range(FREQS):
                    for comp in range(3):
                        re = wide[(f * 2) * 3 + comp, strided(z, v), :]
                        im = wide[(f * 2 + 1) * 3 + comp, strided(z, v), :]
                        turned[f, 0, comp, z, x, v] = keep * (re * ca[f] + im * sa[f])
                        turned[f, 1, comp, z, x, v] = keep * (im * ca[f] - re * sa[f])
            return 0

        return lax.fori_loop(0, SLAB, at_z, 0)

    lax.fori_loop(0, WIDTH, one, 0)


def terms(away, info, e, turned, grad):
    omegas, _, _ = angles()
    z = lax.rem(info[1] + away, SLAB)

    def one(x, _):
        for v in range(HALF):
            total = None
            for comp in range(3):
                plus, minus = [], []
                for i in range(STEPS // 2):
                    lo = e[STEPS // 2 - 1 - i, comp, x, z, v]
                    hi = e[STEPS // 2 + i, comp, x, z, v]
                    plus.append(hi + lo)
                    minus.append(hi - lo)
                for f in range(FREQS):
                    even = odd = None
                    for i in range(STEPS // 2):
                        c = float(np.cos(omegas[f] * (i + 0.5)))
                        s = float(np.sin(omegas[f] * (i + 0.5)))
                        even = c * plus[i] if even is None else even + c * plus[i]
                        odd = s * minus[i] if odd is None else odd + s * minus[i]
                    term = even * turned[f, 0, comp, z, x, v] + odd * turned[f, 1, comp, z, x, v]
                    total = term if total is None else total + term
            grad[x, v] = total
        return 0

    lax.fori_loop(0, WIDTH, one, 0)


def out_kernel(e, h, e_out, h_out):
    def one(x, _):
        for z in range(SLAB):
            for v in range(HALF):
                for comp in range(3):
                    e_out[comp, x, strided(z, v), :] = e[comp, x, z, v]
                    h_out[comp, x, strided(z, v), :] = h[comp, x + 1, z, v] * COEF_H
        return 0

    lax.fori_loop(0, WIDTH, one, 0)


def steps_kernel(
    scale, info, e_all, h_all, coef, inter, intra, late_inter, late_intra, profile,
    e, now, h, over,
    el, hl, er, hr, sums, got, sems,
):
    m = masks()
    odd = lax.rem(info[0], 2)
    hist, tail = pl.ds(0, STEPS), pl.ds(STEPS, DEPTH)
    fetch = []
    for side, early, late in ((odd, inter, late_inter), (1 - odd, intra, late_intra)):
        for src, dst in (
            (early.at[hist], got.at[side, hist]),
            (early.at[tail], got.at[side, pl.ds(2 * STEPS, DEPTH)]),
            (late, got.at[side, pl.ds(STEPS, STEPS)]),
        ):
            fetch.append(pltpu.make_async_copy(src, dst, sems.at[len(fetch)]))
    for copy in fetch:
        copy.start()
    from_left, from_right = got.at[0], got.at[1]

    def place(x, _):
        for comp in range(3):
            now[comp, x] = e_all[comp, x]
            h[comp, x + 1] = h_all[comp, x]
        return 0

    lax.fori_loop(0, WIDTH, place, 0)
    sums[...] = jnp.zeros(sums.shape, jnp.float32)
    for ref in (el, hl, er, hr):
        ref[...] = jnp.zeros(ref.shape, jnp.float32)
    inner = (info[0] > 0).astype(jnp.float32)

    def left(x):
        update_plane(
            el.at[:, x + 1], el.at[:, x + 2], hl.at[:, x + 1], hl.at[:, x],
            from_left.at[2 * STEPS + x], el.at[:, x + 1], m,
        )

    def right(x):
        update_plane(
            er.at[:, x], er.at[:, x + 1], hr.at[:, x + 1], hr.at[:, x],
            from_right.at[2 * STEPS + x], er.at[:, x], m,
        )

    def halos(s):
        el[1:3, DEPTH + 1] = now[1:3, 0]
        blocks = (jnp.minimum(s + 1, STEPS - s) + 1) // 2
        low = DEPTH - 2 * blocks
        sweep(
            blocks,
            lambda i: [(left, low + 2 * i), (right, 2 * i), (left, low + 2 * i + 1), (right, 2 * i + 1)],
            lambda job: job[0](job[1]),
        )

    def step(s, _):
        now[1:3, WIDTH] = er[1:3, 0] + from_right[pl.ds(2 * s - 2, 2)]
        h[1:3, 0] = hl[1:3, DEPTH] * inner + from_left[pl.ds(2 * s - 2, 2)]

        def own(x):
            update_plane(
                now.at[:, x], now.at[:, x + 1], h.at[:, x + 1], h.at[:, x], coef.at[x], now.at[:, x], m,
                e.at[s - 1, :, x], sums.at[s - 1],
            )

        sweep(WIDTH // 4, lambda i: [4 * i + k for k in range(4)], own)
        hr[1:3, 0] = h[1:3, WIDTH]
        halos(s)
        return 0

    for copy in fetch:
        copy.wait()
    halos(0)
    lax.fori_loop(1, STEPS + 1, step, 0)

    omegas = [OMEGA * (f + 1) for f in range(FREQS)]
    profiled = [sum(sums[t, v] * profile[strided(info[2], v), :] for v in range(HALF)) for t in range(STEPS)]
    for f in range(FREQS):
        for q in range(2):
            turn = [float(np.cos(omegas[f] * (t + 1))) if q == 0 else -float(np.sin(omegas[f] * (t + 1))) for t in range(STEPS)]
            val = sum(turn[t] * profiled[t] for t in range(STEPS))
            val = jnp.sum(jnp.sum(val, axis=0, keepdims=True), axis=1, keepdims=True)
            over[2 * f + q : 2 * f + q + 1, :] = jnp.broadcast_to(val * scale, (1, 128))


def finish_kernel(info, e, turned, g0, g1, g2, g3, *scratch):
    grads_far, (*grads, sems) = (g0, g1, g2, g3), scratch
    copies = []
    for away in (1, 2, 3, 0):
        terms(away, info, e, turned, grads[away])
        copies.append(pltpu.make_async_copy(grads[away], grads_far[away], sems.at[away]))
        copies[-1].start()
    for copy in copies:
        copy.wait()


def sum_kernel(a, b, c, d, out):
    for x in range(WIDTH):
        for v in range(HALF):
            out[x, pl.ds(v, 8, stride=2), :] = (a[x, v] + b[x, v]) + (c[x, v] + d[x, v])


def add_kernel(*refs):
    total = refs[0][...]
    for ref in refs[1:-1]:
        total = total + ref[...]
    refs[-1][...] = total


def f32(*shape):
    return jax.ShapeDtypeStruct(shape, jnp.float32)


VMEM = pl.BlockSpec(memory_space=pltpu.VMEM)
SMEM = pl.BlockSpec(memory_space=pltpu.SMEM)
FAR = pl.BlockSpec(memory_space=pltpu.HBM)
ANY = pl.BlockSpec(memory_space=pl.ANY)


def room(mib):
    return pltpu.CompilerParams(vmem_limit_bytes=mib * 1024 * 1024)


def held(*shape):
    return pltpu.VMEM(shape, jnp.float32)


def here(x):
    return pltpu.with_memory_space_constraint(x, pltpu.VMEM)


def far(x):
    return pltpu.with_memory_space_constraint(x, pltpu.HBM)


def body(e_start, h_start, forward, density, material, design, eps_table, profiles, port_mode):
    tiles = lax.axis_size("tile")
    ports = lax.axis_size("port")
    tile = lax.axis_index("tile")
    port = lax.axis_index("port")

    e_rows, h_rows = rows(e_start[0]), rows(h_start[0])
    planes = 2 * STEPS + DEPTH
    half = (3, WIDTH // 2 + 1) + CELLS

    def sent(count):
        return (pltpu.HBM((count, *CELLS), jnp.float32),) * 2

    info = jnp.stack([tile.astype(jnp.int32), port.astype(jnp.int32), port_mode[0]])
    coef, inter, intra, *state = pl.pallas_call(
        free_kernel,
        out_shape=(held(WIDTH, *CELLS),) + sent(STEPS + DEPTH) + (held(*half),) * 4,
        in_specs=[SMEM] * 2 + [FAR] * 5,
        out_specs=(VMEM,) + (FAR,) * 2 + (VMEM,) * 4,
        scratch_shapes=[
            pltpu.VMEM((64, 16), jnp.int32),
            pltpu.VMEM((64, 16), jnp.int32),
            held(WIDTH, 64, 128),
            held(3, WIDTH, 64, 128),
            held(3, WIDTH, 64, 128),
            held(2, STEPS + DEPTH, *CELLS),
            pltpu.SemaphoreType.DMA((5,)),
            pltpu.SemaphoreType.DMA((2,)),
        ],
        compiler_params=room(10),
        name="free",
    )(
        info, far(eps_table), far(material.reshape(64, 16)), far(design.reshape(64, 16)), far(rows(density)),
        far(e_rows), far(h_rows),
    )
    across = [(i, i + 1) for i in range(1, tiles - 1, 2)]

    def swap(inter, intra):
        return (
            lax.ppermute(inter, "tile", across + [(j, i) for i, j in across]),
            lax.ppermute(intra, "tile", [(i, i ^ 1) for i in range(tiles)]),
        )

    inter, intra = swap(inter, intra)
    late_inter, late_intra = pl.pallas_call(
        late_kernel,
        out_shape=sent(STEPS),
        in_specs=[SMEM] + [VMEM] * 5,
        out_specs=(FAR,) * 2,
        scratch_shapes=[held(*half)] * 4 + [held(2, STEPS, *CELLS), pltpu.SemaphoreType.DMA((2,))],
        compiler_params=room(8),
        name="late",
    )(info, here(coef), *[here(x) for x in state])
    blocks, late_inter, late_intra = lax.optimization_barrier((design.reshape(64, 16), late_inter, late_intra))
    late_inter, late_intra = swap(late_inter, late_intra)

    fields = held(3, WIDTH, *CELLS)
    turned, profile, e_all, h_all = pl.pallas_call(
        wide_kernel,
        out_shape=(held(FREQS, 2, 3, SLAB, WIDTH, HALF, 8, 128), f32(64, 128), fields, fields),
        in_specs=[VMEM] * 5,
        out_specs=(VMEM,) * 4,
        scratch_shapes=[held(4 * 3, 64, 128), held(WIDTH, *CELLS)],
        compiler_params=room(4),
        name="wide",
    )(rows(forward[0]), blocks, rows(profiles), e_rows, h_rows)

    scale = 1.0 / math.sqrt(WIDTH * tiles * SLAB * 2048)
    edge = (3, DEPTH + 1) + CELLS
    wider = held(3, WIDTH + 1, *CELLS)
    e_hist, e_last, h_last, over = pl.pallas_call(
        functools.partial(steps_kernel, scale),
        out_shape=(held(STEPS, 3, WIDTH, *CELLS), wider, wider, f32(2 * FREQS, 128)),
        in_specs=[SMEM] + [VMEM] * 3 + [ANY] * 4 + [VMEM],
        out_specs=(VMEM,) * 4,
        scratch_shapes=[
            held(3, DEPTH + 2, *CELLS),
            held(*edge),
            held(*edge),
            held(*edge),
            held(STEPS, HALF, 8, 128),
            held(2, planes, *CELLS),
            pltpu.SemaphoreType.DMA((6,)),
        ],
        compiler_params=room(9),
        name="steps",
    )(info, here(e_all), here(h_all), here(coef), inter, intra, late_inter, late_intra, profile)
    parts = pl.pallas_call(
        finish_kernel,
        out_shape=(pltpu.HBM((WIDTH, HALF, 8, 128), jnp.float32),) * SLAB,
        in_specs=[SMEM, VMEM, VMEM],
        out_specs=(FAR,) * SLAB,
        scratch_shapes=[held(WIDTH, HALF, 8, 128)] * SLAB + [pltpu.SemaphoreType.DMA((SLAB,))],
        compiler_params=room(4),
        name="finish",
    )(info, here(e_hist), here(turned))

    def to_port(x, d):
        return lax.ppermute(x, "port", [(i, (i + d) % ports) for i in range(ports)])

    def stage(total, steps):
        got = []
        for mask in range(1, 1 << len(steps)):
            flip = sum(by for bit, by in enumerate(steps) if mask >> bit & 1)
            got.append(lax.ppermute(total, "tile", [(i, i ^ flip) for i in range(tiles)]))
        return pl.pallas_call(
            add_kernel,
            out_shape=f32(*total.shape),
            in_specs=[VMEM] * (1 + len(got)),
            out_specs=VMEM,
            compiler_params=room(1),
            name="add",
        )(total, *got)

    e_out, h_out = pl.pallas_call(
        out_kernel,
        out_shape=(f32(3, WIDTH, 64, 128), f32(3, WIDTH, 64, 128)),
        in_specs=[VMEM] * 2,
        out_specs=(VMEM,) * 2,
        compiler_params=room(4),
        name="out",
    )(here(e_last), here(h_last))
    total = stage(over, (1, 8))
    total, *parts = lax.optimization_barrier((total, *parts))
    for d in range(1, ports):
        parts[d] = to_port(parts[d], d)
    total = stage(total, (2, 4))
    total, e_out, h_out, *parts = lax.optimization_barrier((total, e_out, h_out, *parts))
    total = stage(total, (16, 32))
    gradient = pl.pallas_call(
        sum_kernel,
        out_shape=f32(WIDTH, 16, 128),
        in_specs=[VMEM] * 4,
        out_specs=VMEM,
        name="total",
    )(*parts)
    return (
        unrows(e_out)[None],
        unrows(h_out)[None],
        gradient.reshape(WIDTH, 1, 2048),
        total[:, 0].reshape(1, FREQS, 2),
    )


def solution(mesh):
    return jax.shard_map(
        body,
        mesh=mesh,
        in_specs=(
            P("port", None, "tile", None, None),
            P("port", None, "tile", None, None),
            P("port", None, None, None, "tile", None, None),
            P("tile", None, None),
            P("tile", None, None),
            P("tile", None, None),
            P(),
            P(),
            P("port"),
        ),
        out_specs=(
            P("port", None, "tile", None, None),
            P("port", None, "tile", None, None),
            P("tile", "port", None),
            P("port", None, None),
        ),
        check_vma=False,
    )
```

```python
import functools
import math

import jax
import jax.numpy as jnp
import numpy as np
from jax import lax
from jax.experimental import pallas as pl
from jax.experimental.pallas import tpu as pltpu
from jax.sharding import PartitionSpec as P

STEPS = 16
OMEGA = 0.7
COEF_H = 0.5
COEF_E = 0.5

WIDTH = 16
SLAB = 4
HALF = 2
ROUND = STEPS // 2
DEPTH = ROUND // 2
FREQS = 2
CELLS = (SLAB, HALF, 8, 128)


def rows(x):
    lead = x.shape[:-2]
    x = x.reshape(lead + (SLAB, 16, 128))
    return jnp.swapaxes(x, -3, -2).reshape(lead + (64, 128))


def unrows(x):
    lead = x.shape[:-2]
    x = x.reshape(lead + (16, SLAB, 128))
    return jnp.swapaxes(x, -3, -2).reshape(lead + (SLAB, 2048))


def masks():
    lane = lax.broadcasted_iota(jnp.int32, (8, 128), 1)
    sub = lax.broadcasted_iota(jnp.int32, (8, 128), 0)
    return lane == 127, lane == 0, sub == 7, sub == 0


def ahead_y(pair, m):
    r0 = pltpu.roll(pair[0], 127, 1)
    r1 = pltpu.roll(pair[1], 127, 1)
    rs = jnp.where(m[2], 0.0, pltpu.roll(r0, 7, 0))
    return jnp.where(m[0], r1, r0), jnp.where(m[0], rs, r1)


def behind_y(pair, m):
    r0 = pltpu.roll(pair[0], 1, 1)
    r1 = pltpu.roll(pair[1], 1, 1)
    rs = jnp.where(m[3], 0.0, pltpu.roll(r1, 1, 0))
    return jnp.where(m[1], rs, r0), jnp.where(m[1], r0, r1)


def update_plane(e_old, e_next, h_now, h_prev, coef, e_new, m, keep=None, sums=None):
    def plane(ref, comp):
        return [[ref[comp, z, v] for v in range(HALF)] for z in range(SLAB)]

    ex, ey, ez = (plane(e_old, comp) for comp in range(3))
    ey_x, ez_x = plane(e_next, 1), plane(e_next, 2)
    hx, hy, hz = (plane(h_now, comp) for comp in range(3))
    hy_x, hz_x = plane(h_prev, 1), plane(h_prev, 2)
    c = [[coef[z, v] for v in range(HALF)] for z in range(SLAB)]
    edge = [0.0] * HALF
    new_e = []
    for z in range(SLAB):
        ex_z, ey_z = (ex[z + 1], ey[z + 1]) if z + 1 < SLAB else (edge, edge)
        ez_y, ex_y = ahead_y(ez[z], m), ahead_y(ex[z], m)
        for v in range(HALF):
            hx[z][v] = hx[z][v] - ((ez_y[v] - ez[z][v]) - (ey_z[v] - ey[z][v]))
            hy[z][v] = hy[z][v] - ((ex_z[v] - ex[z][v]) - (ez_x[z][v] - ez[z][v]))
            hz[z][v] = hz[z][v] - ((ey_x[z][v] - ey[z][v]) - (ex_y[v] - ex[z][v]))
        hz_y, hx_y = behind_y(hz[z], m), behind_y(hx[z], m)
        hx_z, hy_z = (hx[z - 1], hy[z - 1]) if z > 0 else (edge, edge)
        for v in range(HALF):
            curl_x = (hz[z][v] - hz_y[v]) - (hy[z][v] - hy_z[v])
            curl_y = (hx[z][v] - hx_z[v]) - (hz[z][v] - hz_x[z][v])
            curl_z = (hy[z][v] - hy_x[z][v]) - (hx[z][v] - hx_y[v])
            new_e.append(
                (
                    ex[z][v] + c[z][v] * curl_x,
                    ey[z][v] + c[z][v] * curl_y,
                    ez[z][v] + c[z][v] * curl_z,
                )
            )
    for z in range(SLAB):
        for v in range(HALF):
            for comp, h in enumerate((hx, hy, hz)):
                h_now[comp, z, v] = h[z][v]
                e_new[comp, z, v] = new_e[z * HALF + v][comp]
                if keep is not None:
                    keep[comp, z, v] = new_e[z * HALF + v][comp]
    if sums is not None:
        for v in range(HALF):
            sums[v] += sum(new_e[z * HALF + v][1] for z in range(SLAB))


def sweep(blocks, planes, one):
    def block(i, _):
        for plane in planes(i):
            one(plane)
        return 0

    lax.fori_loop(0, blocks, block, 0)


def strided(z, v):
    return pl.ds(4 * v + z, 8, stride=8)


def load_rows(src, dst, scale, first=0, count=WIDTH, base=0):
    def one(x, _):
        for comp in range(3):
            for z in range(SLAB):
                for v in range(HALF):
                    val = src[comp, first + x, strided(z, v), :]
                    dst[comp, base + x, z, v] = val if scale == 1.0 else val * scale
        return 0

    lax.fori_loop(0, count, one, 0)


def by_sublane(ref, v):
    row = lax.broadcasted_iota(jnp.int32, (8, 16), 0)
    col = lax.broadcasted_iota(jnp.int32, (8, 16), 1)
    pick = (col == HALF * row + v).astype(jnp.float32)
    values = ref[...].astype(jnp.float32)
    return lax.dot_general(pick, values, (((1,), (1,)), ((), ())), preferred_element_type=jnp.float32)


def free_run(ea, ha, eb, hb, coef, faces):
    m = masks()
    half = WIDTH // 2
    to_left, to_right = faces.at[0], faces.at[1]
    for e, h in ((ea, ha), (eb, hb)):
        e[:, half] = jnp.zeros((3,) + CELLS, jnp.float32)
        h[:, 0] = jnp.zeros((3,) + CELLS, jnp.float32)

    def low(x):
        update_plane(ea.at[:, x], ea.at[:, x + 1], ha.at[:, x + 1], ha.at[:, x], coef.at[x], ea.at[:, x], m)

    def high(x):
        update_plane(eb.at[:, x], eb.at[:, x + 1], hb.at[:, x + 1], hb.at[:, x], coef.at[half + x], eb.at[:, x], m)

    def step(s, _):
        to_left[pl.ds(2 * s - 2, 2)] = ea[1:3, 0]
        blocks = (ROUND + 2 - s) // 2
        first = half - 2 * blocks
        sweep(
            blocks,
            lambda i: [(low, 2 * i), (high, first + 2 * i), (low, 2 * i + 1), (high, first + 2 * i + 1)],
            lambda job: job[0](job[1]),
        )
        to_right[pl.ds(2 * s - 2, 2)] = hb[1:3, half]
        return 0

    lax.fori_loop(1, ROUND + 1, step, 0)


def swaps(info, faces, inter_far, intra_far, sems):
    odd = lax.rem(info[0], 2)
    return [
        pltpu.make_async_copy(faces.at[side], far, sems.at[i])
        for i, (side, far) in enumerate(((odd, inter_far), (1 - odd, intra_far)))
    ]


def free_kernel(
    info, table, mat_far, des_far, dens_far, e_far, h_far,
    coef, inter_far, intra_far,
    ea, ha, eb, hb, mat, des, dens, e_in, h_in, faces, sems, sent,
):
    to_left, to_right = faces.at[0], faces.at[1]
    pairs = ((mat_far, mat), (des_far, des), (dens_far, dens), (e_far, e_in), (h_far, h_in))
    fetch = [pltpu.make_async_copy(src, dst, sems.at[i]) for i, (src, dst) in enumerate(pairs)]
    for copy in fetch:
        copy.start()
    for copy in fetch[:3]:
        copy.wait()
    for v in range(HALF):
        kind = by_sublane(mat, v)
        flag = by_sublane(des, v)
        base = jnp.zeros(kind.shape, jnp.float32)
        for which in range(table.shape[0]):
            base = base + jnp.where(kind == which, table[which], 0.0)
        for x in range(WIDTH):
            for z in range(SLAB):
                at = x * SLAB + z
                b = jnp.broadcast_to(base[:, at : at + 1], (8, 128))
                d = jnp.broadcast_to(flag[:, at : at + 1], (8, 128))
                eps = b + d * dens[x, strided(z, v), :]
                coef[x, z, v] = (COEF_E * COEF_H) / eps
    to_left[2 * ROUND :] = coef[:DEPTH]
    to_right[2 * ROUND :] = coef[WIDTH - DEPTH :]

    half = WIDTH // 2
    fetch[3].wait()
    fetch[4].wait()
    load_rows(e_in, ea, 1.0, 0, half)
    load_rows(e_in, eb, 1.0, half, half)
    load_rows(h_in, ha, 1.0 / COEF_H, 0, half, 1)
    load_rows(h_in, hb, 1.0 / COEF_H, half, half, 1)
    free_run(ea, ha, eb, hb, coef, faces)
    sends = swaps(info, faces, inter_far, intra_far, sent)
    for copy in sends:
        copy.start()
    for copy in sends:
        copy.wait()


def angles():
    omegas = [OMEGA * (f + 1) for f in range(FREQS)]
    mid = (ROUND + 1) / 2
    return omegas, [float(np.cos(w * mid)) for w in omegas], [float(np.sin(w * mid)) for w in omegas]


def wide_kernel(forward, des, profile_in, e_in, h_in, turned, profile, e_all, h_all, wide, mask):
    _, ca, sa = angles()
    profile[...] = profile_in[...]
    for v in range(HALF):
        flag = by_sublane(des, v)
        for x in range(WIDTH):
            for z in range(SLAB):
                at = x * SLAB + z
                mask[x, z, v] = jnp.broadcast_to(flag[:, at : at + 1], (8, 128)) * (1.0 / STEPS)
    load_rows(e_in, e_all, 1.0)
    load_rows(h_in, h_all, 1.0 / COEF_H, base=1)

    def one(x, _):
        for f in range(FREQS):
            for q in range(2):
                for comp in range(3):
                    wide[(f * 2 + q) * 3 + comp] = forward[f, q, comp, x].astype(jnp.float32)

        def at_z(z, _):
            for v in range(HALF):
                keep = mask[x, z, v]
                for f in range(FREQS):
                    for comp in range(3):
                        re = wide[(f * 2) * 3 + comp, strided(z, v), :]
                        im = wide[(f * 2 + 1) * 3 + comp, strided(z, v), :]
                        turned[f, 0, comp, z, x, v] = keep * (re * ca[f] + im * sa[f])
                        turned[f, 1, comp, z, x, v] = keep * (im * ca[f] - re * sa[f])
            return 0

        return lax.fori_loop(0, SLAB, at_z, 0)

    lax.fori_loop(0, WIDTH, one, 0)


def terms(e, turned, x, z, v):
    omegas, _, _ = angles()
    total = None
    for comp in range(3):
        plus, minus = [], []
        for i in range(ROUND // 2):
            lo = e[ROUND // 2 - 1 - i, comp, x, z, v]
            hi = e[ROUND // 2 + i, comp, x, z, v]
            plus.append(hi + lo)
            minus.append(hi - lo)
        for f in range(FREQS):
            even = odd = None
            for i in range(ROUND // 2):
                c = float(np.cos(omegas[f] * (i + 0.5)))
                s = float(np.sin(omegas[f] * (i + 0.5)))
                even = c * plus[i] if even is None else even + c * plus[i]
                odd = s * minus[i] if odd is None else odd + s * minus[i]
            term = even * turned[f, 0, comp, z, x, v] + odd * turned[f, 1, comp, z, x, v]
            total = term if total is None else total + term
    return total


def first_kernel(e, turned, grad, later):
    omegas, _, _ = angles()

    def one(x, _):
        def at_z(z, _):
            for v in range(HALF):
                grad[z, x, v] = terms(e, turned, x, z, v)
                for f in range(FREQS):
                    c, s = float(np.cos(omegas[f] * ROUND)), float(np.sin(omegas[f] * ROUND))
                    for comp in range(3):
                        re, im = turned[f, 0, comp, z, x, v], turned[f, 1, comp, z, x, v]
                        later[f, 0, comp, z, x, v] = c * re + s * im
                        later[f, 1, comp, z, x, v] = c * im - s * re
            return 0

        return lax.fori_loop(0, SLAB, at_z, 0)

    lax.fori_loop(0, WIDTH, one, 0)


def out_kernel(e, h, e_out, h_out):
    def one(x, _):
        for z in range(SLAB):
            for v in range(HALF):
                for comp in range(3):
                    e_out[comp, x, strided(z, v), :] = e[comp, x, z, v]
                    h_out[comp, x, strided(z, v), :] = h[comp, x + 1, z, v] * COEF_H
        return 0

    lax.fori_loop(0, WIDTH, one, 0)


def round_kernel(final, scale, info, e_in, h_in, coef, inter, intra, *rest):
    if final:
        (late_inter, late_intra, profile, sums_before), rest = rest[:4], rest[4:]
        (e, now, h, over), (el, hl, er, hr, got, sems, sums) = rest[:4], rest[4:]
    else:
        (e, now, h, sums, inter_far, intra_far), rest = rest[:6], rest[6:]
        el, hl, er, hr, got, sems, ea, ha, eb, hb, faces, sent = rest
        late_inter, late_intra = inter, intra
    m = masks()
    odd = lax.rem(info[0], 2)
    hist, tail = pl.ds(0, 2 * ROUND), pl.ds(2 * ROUND, DEPTH)
    fetch = []
    for side, early, late in ((odd, inter, late_inter), (1 - odd, intra, late_intra)):
        for src, part in ((late, hist), (early, tail)):
            fetch.append(pltpu.make_async_copy(src.at[part], got.at[side, part], sems.at[len(fetch)]))
    for copy in fetch:
        copy.start()
    from_left, from_right = got.at[0], got.at[1]

    def place(x, _):
        for comp in range(3):
            now[comp, x] = e_in[comp, x]
            h[comp, x + 1] = h_in[comp, x + 1]
        return 0

    lax.fori_loop(0, WIDTH, place, 0)
    sums[...] = jnp.zeros(sums.shape, jnp.float32)
    for ref in (el, hl, er, hr):
        ref[...] = jnp.zeros(ref.shape, jnp.float32)
    inner = (info[0] > 0).astype(jnp.float32)

    def left(x):
        update_plane(
            el.at[:, x + 1], el.at[:, x + 2], hl.at[:, x + 1], hl.at[:, x],
            from_left.at[2 * ROUND + x], el.at[:, x + 1], m,
        )

    def right(x):
        update_plane(
            er.at[:, x], er.at[:, x + 1], hr.at[:, x + 1], hr.at[:, x],
            from_right.at[2 * ROUND + x], er.at[:, x], m,
        )

    def halos(s):
        el[1:3, DEPTH + 1] = now[1:3, 0]
        blocks = (jnp.minimum(s + 1, ROUND - s) + 1) // 2
        low = DEPTH - 2 * blocks
        sweep(
            blocks,
            lambda i: [(left, low + 2 * i), (right, 2 * i), (left, low + 2 * i + 1), (right, 2 * i + 1)],
            lambda job: job[0](job[1]),
        )

    def step(s, _):
        now[1:3, WIDTH] = er[1:3, 0] + from_right[pl.ds(2 * s - 2, 2)]
        h[1:3, 0] = hl[1:3, DEPTH] * inner + from_left[pl.ds(2 * s - 2, 2)]

        def own(x):
            update_plane(
                now.at[:, x], now.at[:, x + 1], h.at[:, x + 1], h.at[:, x], coef.at[x], now.at[:, x], m,
                e.at[s - 1, :, x], sums.at[s - 1],
            )

        sweep(WIDTH // 4, lambda i: [4 * i + k for k in range(4)], own)
        hr[1:3, 0] = h[1:3, WIDTH]
        halos(s)
        return 0

    for copy in fetch:
        copy.wait()
    halos(0)
    lax.fori_loop(1, ROUND + 1, step, 0)

    if not final:
        half = WIDTH // 2

        def split(x, _):
            for comp in range(3):
                ea[comp, x] = now[comp, x]
                eb[comp, x] = now[comp, half + x]
                ha[comp, x + 1] = h[comp, x + 1]
                hb[comp, x + 1] = h[comp, half + x + 1]
            return 0

        lax.fori_loop(0, half, split, 0)
        free_run(ea, ha, eb, hb, coef, faces)
        sends = swaps(info, faces, inter_far, intra_far, sent)
        for copy in sends:
            copy.start()
        for copy in sends:
            copy.wait()
        return

    omegas, _, _ = angles()
    profiled = [
        sum(ref[t, v] * profile[strided(info[2], v), :] for v in range(HALF))
        for ref in (sums_before, sums)
        for t in range(ROUND)
    ]
    for f in range(FREQS):
        for q, turn in enumerate((np.cos, lambda angle: -np.sin(angle))):
            val = sum(float(turn(omegas[f] * (t + 1))) * profiled[t] for t in range(STEPS))
            val = jnp.sum(jnp.sum(val, axis=0, keepdims=True), axis=1, keepdims=True)
            over[2 * f + q : 2 * f + q + 1, :] = jnp.broadcast_to(val * scale, (1, 128))


def finish_kernel(info, e, turned, before, g0, g1, g2, g3, *scratch):
    grads_far, (*grads, sems) = (g0, g1, g2, g3), scratch
    copies = []
    for away in (1, 2, 3, 0):
        z = lax.rem(info[1] + away, SLAB)

        def one(x, _, grad=grads[away], z=z):
            for v in range(HALF):
                grad[x, v] = before[z, x, v] + terms(e, turned, x, z, v)
            return 0

        lax.fori_loop(0, WIDTH, one, 0)
        copies.append(pltpu.make_async_copy(grads[away], grads_far[away], sems.at[away]))
        copies[-1].start()
    for copy in copies:
        copy.wait()


def sum_kernel(a, b, c, d, out):
    for x in range(WIDTH):
        for v in range(HALF):
            out[x, pl.ds(v, 8, stride=2), :] = (a[x, v] + b[x, v]) + (c[x, v] + d[x, v])


def add_kernel(*refs):
    total = refs[0][...]
    for ref in refs[1:-1]:
        total = total + ref[...]
    refs[-1][...] = total


def last_kernel(*refs):
    total = refs[0][...]
    for ref in refs[1:-1]:
        total = total + ref[...]
    lane = lax.broadcasted_iota(jnp.int32, (1, 128), 1)
    for f in range(FREQS):
        both = jnp.where(lane == 0, total[2 * f : 2 * f + 1], total[2 * f + 1 : 2 * f + 2])
        refs[-1][0, f : f + 1, :] = both[:, :2]


def f32(*shape):
    return jax.ShapeDtypeStruct(shape, jnp.float32)


VMEM = pl.BlockSpec(memory_space=pltpu.VMEM)
SMEM = pl.BlockSpec(memory_space=pltpu.SMEM)
FAR = pl.BlockSpec(memory_space=pltpu.HBM)
ANY = pl.BlockSpec(memory_space=pl.ANY)


def room(mib):
    return pltpu.CompilerParams(vmem_limit_bytes=mib * 1024 * 1024)


def held(*shape):
    return pltpu.VMEM(shape, jnp.float32)


def here(x):
    return pltpu.with_memory_space_constraint(x, pltpu.VMEM)


def far(x):
    return pltpu.with_memory_space_constraint(x, pltpu.HBM)


def body(e_start, h_start, forward, density, material, design, eps_table, profiles, port_mode):
    tiles = lax.axis_size("tile")
    ports = lax.axis_size("port")
    tile = lax.axis_index("tile")
    port = lax.axis_index("port")

    e_rows, h_rows = rows(e_start[0]), rows(h_start[0])
    planes = 2 * ROUND + DEPTH
    half = (3, WIDTH // 2 + 1) + CELLS

    def sent(count):
        return (pltpu.HBM((count, *CELLS), jnp.float32),) * 2

    info = jnp.stack([tile.astype(jnp.int32), port.astype(jnp.int32), port_mode[0]])
    coef, inter, intra = pl.pallas_call(
        free_kernel,
        out_shape=(f32(WIDTH, *CELLS),) + sent(planes),
        in_specs=[SMEM] * 2 + [FAR] * 5,
        out_specs=(VMEM,) + (FAR,) * 2,
        scratch_shapes=[held(*half)] * 4
        + [
            pltpu.VMEM((64, 16), jnp.int32),
            pltpu.VMEM((64, 16), jnp.int32),
            held(WIDTH, 64, 128),
            held(3, WIDTH, 64, 128),
            held(3, WIDTH, 64, 128),
            held(2, planes, *CELLS),
            pltpu.SemaphoreType.DMA((5,)),
            pltpu.SemaphoreType.DMA((2,)),
        ],
        compiler_params=room(12),
        name="free",
    )(
        info, far(eps_table), far(material.reshape(64, 16)), far(design.reshape(64, 16)), far(rows(density)),
        far(e_rows), far(h_rows),
    )
    across = [(i, i + 1) for i in range(1, tiles - 1, 2)]

    def swap(inter, intra):
        return (
            lax.ppermute(inter, "tile", across + [(j, i) for i, j in across]),
            lax.ppermute(intra, "tile", [(i, i ^ 1) for i in range(tiles)]),
        )

    blocks, inter, intra = lax.optimization_barrier((design.reshape(64, 16), inter, intra))
    inter, intra = swap(inter, intra)

    fields = held(3, WIDTH + 1, *CELLS)
    turned_shape = held(FREQS, 2, 3, SLAB, WIDTH, HALF, 8, 128)
    turned, profile, e_all, h_all = pl.pallas_call(
        wide_kernel,
        out_shape=(turned_shape, f32(64, 128), fields, fields),
        in_specs=[VMEM] * 5,
        out_specs=(VMEM,) * 4,
        scratch_shapes=[held(4 * 3, 64, 128), held(WIDTH, *CELLS)],
        compiler_params=room(4),
        name="wide",
    )(rows(forward[0]), blocks, rows(profiles), e_rows, h_rows)

    scale = 1.0 / math.sqrt(WIDTH * tiles * SLAB * 2048)
    edge = (3, DEPTH + 1) + CELLS
    history = held(ROUND, 3, WIDTH, *CELLS)
    halos = [
        held(3, DEPTH + 2, *CELLS),
        held(*edge),
        held(*edge),
        held(*edge),
        held(2, planes, *CELLS),
        pltpu.SemaphoreType.DMA((4,)),
    ]
    e_first, e_mid, h_mid, sums, late_inter, late_intra = pl.pallas_call(
        functools.partial(round_kernel, False, scale),
        out_shape=(history, fields, fields, f32(ROUND, HALF, 8, 128)) + sent(2 * ROUND),
        in_specs=[SMEM] + [VMEM] * 3 + [ANY] * 2,
        out_specs=(VMEM,) * 4 + (FAR,) * 2,
        scratch_shapes=halos
        + [held(*half)] * 4
        + [held(2, 2 * ROUND, *CELLS), pltpu.SemaphoreType.DMA((2,))],
        compiler_params=room(12),
        name="round",
    )(info, here(e_all), here(h_all), coef, inter, intra)
    late_inter, late_intra = swap(late_inter, late_intra)
    grad_first, turned = pl.pallas_call(
        first_kernel,
        out_shape=(f32(SLAB, WIDTH, HALF, 8, 128), turned_shape),
        in_specs=[VMEM] * 2,
        out_specs=(VMEM,) * 2,
        compiler_params=room(2),
        name="first",
    )(here(e_first), here(turned))
    sums, grad_first = lax.optimization_barrier((sums, grad_first))
    e_second, e_last, h_last, over = pl.pallas_call(
        functools.partial(round_kernel, True, scale),
        out_shape=(history, fields, fields, f32(2 * FREQS, 128)),
        in_specs=[SMEM] + [VMEM] * 3 + [ANY] * 4 + [VMEM] * 2,
        out_specs=(VMEM,) * 4,
        scratch_shapes=halos + [held(ROUND, HALF, 8, 128)],
        compiler_params=room(8),
        name="round",
    )(info, here(e_mid), here(h_mid), coef, inter, intra, late_inter, late_intra, profile, sums)
    parts = pl.pallas_call(
        finish_kernel,
        out_shape=(pltpu.HBM((WIDTH, HALF, 8, 128), jnp.float32),) * SLAB,
        in_specs=[SMEM] + [VMEM] * 3,
        out_specs=(FAR,) * SLAB,
        scratch_shapes=[held(WIDTH, HALF, 8, 128)] * SLAB + [pltpu.SemaphoreType.DMA((SLAB,))],
        compiler_params=room(4),
        name="finish",
    )(info, here(e_second), here(turned), grad_first)

    def to_port(x, d):
        return lax.ppermute(x, "port", [(i, (i + d) % ports) for i in range(ports)])

    def stage(total, steps, kernel=add_kernel, shape=(2 * FREQS, 128)):
        got = []
        for mask in range(1, 1 << len(steps)):
            flip = sum(by for bit, by in enumerate(steps) if mask >> bit & 1)
            got.append(lax.ppermute(total, "tile", [(i, i ^ flip) for i in range(tiles)]))
        return pl.pallas_call(
            kernel,
            out_shape=f32(*shape),
            in_specs=[VMEM] * (1 + len(got)),
            out_specs=VMEM,
            compiler_params=room(1),
            name="add",
        )(total, *got)

    e_out, h_out = pl.pallas_call(
        out_kernel,
        out_shape=(f32(3, WIDTH, 64, 128), f32(3, WIDTH, 64, 128)),
        in_specs=[VMEM] * 2,
        out_specs=(VMEM,) * 2,
        compiler_params=room(4),
        name="out",
    )(here(e_last), here(h_last))
    total = stage(over, (1, 8))
    total, *parts = lax.optimization_barrier((total, *parts))
    for d in range(1, ports):
        parts[d] = to_port(parts[d], d)
    total = stage(total, (2, 4))
    total, e_out, h_out, *parts = lax.optimization_barrier((total, e_out, h_out, *parts))
    intersections = stage(total, (16, 32), last_kernel, (1, FREQS, 2))
    gradient = pl.pallas_call(
        sum_kernel,
        out_shape=f32(WIDTH, 16, 128),
        in_specs=[VMEM] * 4,
        out_specs=VMEM,
        name="total",
    )(*parts)
    return (
        unrows(e_out)[None],
        unrows(h_out)[None],
        gradient.reshape(WIDTH, 1, 2048),
        intersections,
    )


def solution(mesh):
    return jax.shard_map(
        body,
        mesh=mesh,
        in_specs=(
            P("port", None, "tile", None, None),
            P("port", None, "tile", None, None),
            P("port", None, None, None, "tile", None, None),
            P("tile", None, None),
            P("tile", None, None),
            P("tile", None, None),
            P(),
            P(),
            P("port"),
        ),
        out_specs=(
            P("port", None, "tile", None, None),
            P("port", None, "tile", None, None),
            P("tile", "port", None),
            P("port", None, None),
        ),
        check_vma=False,
    )
```

```python
import functools
import math

import jax
import jax.numpy as jnp
import numpy as np
from jax import lax
from jax.experimental import pallas as pl
from jax.experimental.pallas import tpu as pltpu
from jax.sharding import PartitionSpec as P

STEPS = 16
OMEGA = 0.7
COEF_H = 0.5
COEF_E = 0.5

WIDTH = 16
SLAB = 4
HALF = 2
ROUND = STEPS // 2
DEPTH = ROUND // 2
FREQS = 2
CELLS = (SLAB, HALF, 8, 128)


def rows(x):
    lead = x.shape[:-2]
    x = x.reshape(lead + (SLAB, 16, 128))
    return jnp.swapaxes(x, -3, -2).reshape(lead + (64, 128))


def unrows(x):
    lead = x.shape[:-2]
    x = x.reshape(lead + (16, SLAB, 128))
    return jnp.swapaxes(x, -3, -2).reshape(lead + (SLAB, 2048))


def masks():
    lane = lax.broadcasted_iota(jnp.int32, (8, 128), 1)
    sub = lax.broadcasted_iota(jnp.int32, (8, 128), 0)
    return lane == 127, lane == 0, sub == 7, sub == 0


def ahead_y(pair, m):
    r0 = pltpu.roll(pair[0], 127, 1)
    r1 = pltpu.roll(pair[1], 127, 1)
    rs = jnp.where(m[2], 0.0, pltpu.roll(r0, 7, 0))
    return jnp.where(m[0], r1, r0), jnp.where(m[0], rs, r1)


def behind_y(pair, m):
    r0 = pltpu.roll(pair[0], 1, 1)
    r1 = pltpu.roll(pair[1], 1, 1)
    rs = jnp.where(m[3], 0.0, pltpu.roll(r1, 1, 0))
    return jnp.where(m[1], rs, r0), jnp.where(m[1], r0, r1)


def update_plane(e_old, e_next, h_now, h_prev, coef, e_new, m, keep=None, sums=None):
    def plane(ref, comp):
        return [[ref[comp, z, v] for v in range(HALF)] for z in range(SLAB)]

    ex, ey, ez = (plane(e_old, comp) for comp in range(3))
    ey_x, ez_x = plane(e_next, 1), plane(e_next, 2)
    hx, hy, hz = (plane(h_now, comp) for comp in range(3))
    hy_x, hz_x = plane(h_prev, 1), plane(h_prev, 2)
    c = [[coef[z, v] for v in range(HALF)] for z in range(SLAB)]
    edge = [0.0] * HALF
    new_e = []
    for z in range(SLAB):
        ex_z, ey_z = (ex[z + 1], ey[z + 1]) if z + 1 < SLAB else (edge, edge)
        ez_y, ex_y = ahead_y(ez[z], m), ahead_y(ex[z], m)
        for v in range(HALF):
            hx[z][v] = hx[z][v] - ((ez_y[v] - ez[z][v]) - (ey_z[v] - ey[z][v]))
            hy[z][v] = hy[z][v] - ((ex_z[v] - ex[z][v]) - (ez_x[z][v] - ez[z][v]))
            hz[z][v] = hz[z][v] - ((ey_x[z][v] - ey[z][v]) - (ex_y[v] - ex[z][v]))
        hz_y, hx_y = behind_y(hz[z], m), behind_y(hx[z], m)
        hx_z, hy_z = (hx[z - 1], hy[z - 1]) if z > 0 else (edge, edge)
        for v in range(HALF):
            curl_x = (hz[z][v] - hz_y[v]) - (hy[z][v] - hy_z[v])
            curl_y = (hx[z][v] - hx_z[v]) - (hz[z][v] - hz_x[z][v])
            curl_z = (hy[z][v] - hy_x[z][v]) - (hx[z][v] - hx_y[v])
            new_e.append(
                (
                    ex[z][v] + c[z][v] * curl_x,
                    ey[z][v] + c[z][v] * curl_y,
                    ez[z][v] + c[z][v] * curl_z,
                )
            )
    for z in range(SLAB):
        for v in range(HALF):
            for comp, h in enumerate((hx, hy, hz)):
                h_now[comp, z, v] = h[z][v]
                e_new[comp, z, v] = new_e[z * HALF + v][comp]
                if keep is not None:
                    keep[comp, z, v] = new_e[z * HALF + v][comp]
    if sums is not None:
        for v in range(HALF):
            sums[v] += sum(new_e[z * HALF + v][1] for z in range(SLAB))


def sweep(blocks, planes, one):
    def block(i, _):
        for plane in planes(i):
            one(plane)
        return 0

    lax.fori_loop(0, blocks, block, 0)


def strided(z, v):
    return pl.ds(4 * v + z, 8, stride=8)


def load_rows(src, dst, scale, first=0, count=WIDTH, base=0):
    def one(x, _):
        for comp in range(3):
            for z in range(SLAB):
                for v in range(HALF):
                    val = src[comp, first + x, strided(z, v), :]
                    dst[comp, base + x, z, v] = val if scale == 1.0 else val * scale
        return 0

    lax.fori_loop(0, count, one, 0)


def by_sublane(ref, v):
    row = lax.broadcasted_iota(jnp.int32, (8, 16), 0)
    col = lax.broadcasted_iota(jnp.int32, (8, 16), 1)
    pick = (col == HALF * row + v).astype(jnp.float32)
    values = ref[...].astype(jnp.float32)
    return lax.dot_general(pick, values, (((1,), (1,)), ((), ())), preferred_element_type=jnp.float32)


def free_run(ea, ha, eb, hb, coef, faces, sends):
    m = masks()
    half = WIDTH // 2
    to_left, to_right = faces.at[0], faces.at[1]
    for e, h in ((ea, ha), (eb, hb)):
        e[:, half] = jnp.zeros((3,) + CELLS, jnp.float32)
        h[:, 0] = jnp.zeros((3,) + CELLS, jnp.float32)

    def low(x):
        update_plane(ea.at[:, x], ea.at[:, x + 1], ha.at[:, x + 1], ha.at[:, x], coef.at[x], ea.at[:, x], m)

    def high(x):
        update_plane(eb.at[:, x], eb.at[:, x + 1], hb.at[:, x + 1], hb.at[:, x], coef.at[half + x], eb.at[:, x], m)

    def step(s, _):
        to_left[pl.ds(2 * s - 2, 2)] = ea[1:3, 0]
        blocks = (ROUND + 2 - s) // 2
        first = half - 2 * blocks
        sweep(
            blocks,
            lambda i: [(low, 2 * i), (high, first + 2 * i), (low, 2 * i + 1), (high, first + 2 * i + 1)],
            lambda job: job[0](job[1]),
        )
        to_right[pl.ds(2 * s - 2, 2)] = hb[1:3, half]
        return 0

    lax.fori_loop(1, ROUND // 2 + 1, step, 0)
    for copy in sends[:2]:
        copy.start()
    lax.fori_loop(ROUND // 2 + 1, ROUND + 1, step, 0)
    for copy in sends[2:]:
        copy.start()
    for copy in sends:
        copy.wait()


def swaps(info, faces, inter_far, intra_far, sems):
    odd = lax.rem(info[0], 2)
    copies = []
    for part in (pl.ds(0, ROUND), pl.ds(ROUND, faces.shape[1] - ROUND)):
        for side, far in ((odd, inter_far), (1 - odd, intra_far)):
            copies.append(pltpu.make_async_copy(faces.at[side, part], far.at[part], sems.at[len(copies)]))
    return copies


def free_kernel(
    info, table, mat_far, des_far, dens_far, e_far, h_far,
    coef, inter_far, intra_far,
    ea, ha, eb, hb, mat, des, dens, e_in, h_in, faces, sems, sent,
):
    to_left, to_right = faces.at[0], faces.at[1]
    pairs = ((mat_far, mat), (des_far, des), (dens_far, dens), (e_far, e_in), (h_far, h_in))
    fetch = [pltpu.make_async_copy(src, dst, sems.at[i]) for i, (src, dst) in enumerate(pairs)]
    for copy in fetch:
        copy.start()
    for copy in fetch[:3]:
        copy.wait()
    for v in range(HALF):
        kind = by_sublane(mat, v)
        flag = by_sublane(des, v)
        base = jnp.zeros(kind.shape, jnp.float32)
        for which in range(table.shape[0]):
            base = base + jnp.where(kind == which, table[which], 0.0)
        for x in range(WIDTH):
            for z in range(SLAB):
                at = x * SLAB + z
                b = jnp.broadcast_to(base[:, at : at + 1], (8, 128))
                d = jnp.broadcast_to(flag[:, at : at + 1], (8, 128))
                eps = b + d * dens[x, strided(z, v), :]
                coef[x, z, v] = (COEF_E * COEF_H) / eps
    to_left[2 * ROUND :] = coef[:DEPTH]
    to_right[2 * ROUND :] = coef[WIDTH - DEPTH :]

    half = WIDTH // 2
    fetch[3].wait()
    fetch[4].wait()
    load_rows(e_in, ea, 1.0, 0, half)
    load_rows(e_in, eb, 1.0, half, half)
    load_rows(h_in, ha, 1.0 / COEF_H, 0, half, 1)
    load_rows(h_in, hb, 1.0 / COEF_H, half, half, 1)
    free_run(ea, ha, eb, hb, coef, faces, swaps(info, faces, inter_far, intra_far, sent))


def angles():
    omegas = [OMEGA * (f + 1) for f in range(FREQS)]
    mid = (ROUND + 1) / 2
    return omegas, [float(np.cos(w * mid)) for w in omegas], [float(np.sin(w * mid)) for w in omegas]


def wide_kernel(forward, des, profile_in, e_in, h_in, turned, profile, e_all, h_all, wide, mask):
    _, ca, sa = angles()
    profile[...] = profile_in[...]
    for v in range(HALF):
        flag = by_sublane(des, v)
        for x in range(WIDTH):
            for z in range(SLAB):
                at = x * SLAB + z
                mask[x, z, v] = jnp.broadcast_to(flag[:, at : at + 1], (8, 128)) * (1.0 / STEPS)
    load_rows(e_in, e_all, 1.0)
    load_rows(h_in, h_all, 1.0 / COEF_H, base=1)

    def one(x, _):
        for f in range(FREQS):
            for q in range(2):
                for comp in range(3):
                    wide[(f * 2 + q) * 3 + comp] = forward[f, q, comp, x].astype(jnp.float32)

        def at_z(z, _):
            for v in range(HALF):
                keep = mask[x, z, v]
                for f in range(FREQS):
                    for comp in range(3):
                        re = wide[(f * 2) * 3 + comp, strided(z, v), :]
                        im = wide[(f * 2 + 1) * 3 + comp, strided(z, v), :]
                        turned[f, 0, comp, z, x, v] = keep * (re * ca[f] + im * sa[f])
                        turned[f, 1, comp, z, x, v] = keep * (im * ca[f] - re * sa[f])
            return 0

        return lax.fori_loop(0, SLAB, at_z, 0)

    lax.fori_loop(0, WIDTH, one, 0)


def terms(e, turned, x, z, v):
    omegas, _, _ = angles()
    total = None
    for comp in range(3):
        plus, minus = [], []
        for i in range(ROUND // 2):
            lo = e[ROUND // 2 - 1 - i, comp, x, z, v]
            hi = e[ROUND // 2 + i, comp, x, z, v]
            plus.append(hi + lo)
            minus.append(hi - lo)
        for f in range(FREQS):
            even = odd = None
            for i in range(ROUND // 2):
                c = float(np.cos(omegas[f] * (i + 0.5)))
                s = float(np.sin(omegas[f] * (i + 0.5)))
                even = c * plus[i] if even is None else even + c * plus[i]
                odd = s * minus[i] if odd is None else odd + s * minus[i]
            term = even * turned[f, 0, comp, z, x, v] + odd * turned[f, 1, comp, z, x, v]
            total = term if total is None else total + term
    return total


def first_kernel(e, turned, grad, later):
    omegas, _, _ = angles()

    def one(x, _):
        def at_z(z, _):
            for v in range(HALF):
                grad[z, x, v] = terms(e, turned, x, z, v)
                for f in range(FREQS):
                    c, s = float(np.cos(omegas[f] * ROUND)), float(np.sin(omegas[f] * ROUND))
                    for comp in range(3):
                        re, im = turned[f, 0, comp, z, x, v], turned[f, 1, comp, z, x, v]
                        later[f, 0, comp, z, x, v] = c * re + s * im
                        later[f, 1, comp, z, x, v] = c * im - s * re
            return 0

        return lax.fori_loop(0, SLAB, at_z, 0)

    lax.fori_loop(0, WIDTH, one, 0)


def out_kernel(e, h, e_out, h_out):
    def one(x, _):
        for z in range(SLAB):
            for v in range(HALF):
                for comp in range(3):
                    e_out[comp, x, strided(z, v), :] = e[comp, x, z, v]
                    h_out[comp, x, strided(z, v), :] = h[comp, x + 1, z, v] * COEF_H
        return 0

    lax.fori_loop(0, WIDTH, one, 0)


def round_kernel(final, scale, info, e_in, h_in, coef, inter, intra, *rest):
    if final:
        (late_inter, late_intra, profile, sums_before), rest = rest[:4], rest[4:]
        (e, now, h, over), (el, hl, er, hr, got, sems, sums) = rest[:4], rest[4:]
    else:
        (e, now, h, sums, inter_far, intra_far), rest = rest[:6], rest[6:]
        el, hl, er, hr, got, sems, ea, ha, eb, hb, faces, sent = rest
        late_inter, late_intra = inter, intra
    m = masks()
    odd = lax.rem(info[0], 2)
    hist, tail = pl.ds(0, 2 * ROUND), pl.ds(2 * ROUND, DEPTH)
    fetch = []
    for side, early, late in ((odd, inter, late_inter), (1 - odd, intra, late_intra)):
        for src, part in ((late, hist), (early, tail)):
            fetch.append(pltpu.make_async_copy(src.at[part], got.at[side, part], sems.at[len(fetch)]))
    for copy in fetch:
        copy.start()
    from_left, from_right = got.at[0], got.at[1]

    def place(x, _):
        for comp in range(3):
            now[comp, x] = e_in[comp, x]
            h[comp, x + 1] = h_in[comp, x + 1]
        return 0

    lax.fori_loop(0, WIDTH, place, 0)
    sums[...] = jnp.zeros(sums.shape, jnp.float32)
    for ref in (el, hl, er, hr):
        ref[...] = jnp.zeros(ref.shape, jnp.float32)
    inner = (info[0] > 0).astype(jnp.float32)

    def left(x):
        update_plane(
            el.at[:, x + 1], el.at[:, x + 2], hl.at[:, x + 1], hl.at[:, x],
            from_left.at[2 * ROUND + x], el.at[:, x + 1], m,
        )

    def right(x):
        update_plane(
            er.at[:, x], er.at[:, x + 1], hr.at[:, x + 1], hr.at[:, x],
            from_right.at[2 * ROUND + x], er.at[:, x], m,
        )

    def halos(s):
        el[1:3, DEPTH + 1] = now[1:3, 0]
        blocks = (jnp.minimum(s + 1, ROUND - s) + 1) // 2
        low = DEPTH - 2 * blocks
        sweep(
            blocks,
            lambda i: [(left, low + 2 * i), (right, 2 * i), (left, low + 2 * i + 1), (right, 2 * i + 1)],
            lambda job: job[0](job[1]),
        )

    def step(s, _):
        now[1:3, WIDTH] = er[1:3, 0] + from_right[pl.ds(2 * s - 2, 2)]
        h[1:3, 0] = hl[1:3, DEPTH] * inner + from_left[pl.ds(2 * s - 2, 2)]

        def own(x):
            update_plane(
                now.at[:, x], now.at[:, x + 1], h.at[:, x + 1], h.at[:, x], coef.at[x], now.at[:, x], m,
                e.at[s - 1, :, x], sums.at[s - 1],
            )

        sweep(WIDTH // 4, lambda i: [4 * i + k for k in range(4)], own)
        hr[1:3, 0] = h[1:3, WIDTH]
        halos(s)
        return 0

    for copy in fetch:
        copy.wait()
    halos(0)
    lax.fori_loop(1, ROUND + 1, step, 0)

    if not final:
        half = WIDTH // 2

        def split(x, _):
            for comp in range(3):
                ea[comp, x] = now[comp, x]
                eb[comp, x] = now[comp, half + x]
                ha[comp, x + 1] = h[comp, x + 1]
                hb[comp, x + 1] = h[comp, half + x + 1]
            return 0

        lax.fori_loop(0, half, split, 0)
        free_run(ea, ha, eb, hb, coef, faces, swaps(info, faces, inter_far, intra_far, sent))
        return

    omegas, _, _ = angles()
    profiled = [
        sum(ref[t, v] * profile[strided(info[2], v), :] for v in range(HALF))
        for ref in (sums_before, sums)
        for t in range(ROUND)
    ]
    for f in range(FREQS):
        for q, turn in enumerate((np.cos, lambda angle: -np.sin(angle))):
            val = sum(float(turn(omegas[f] * (t + 1))) * profiled[t] for t in range(STEPS))
            val = jnp.sum(jnp.sum(val, axis=0, keepdims=True), axis=1, keepdims=True)
            over[2 * f + q : 2 * f + q + 1, :] = jnp.broadcast_to(val * scale, (1, 128))


def finish_kernel(info, e, turned, before, g0, g1, g2, g3, *scratch):
    grads_far, (*grads, sems) = (g0, g1, g2, g3), scratch
    copies = []
    for away in (1, 2, 3, 0):
        z = lax.rem(info[1] + away, SLAB)

        def one(x, _, grad=grads[away], z=z):
            for v in range(HALF):
                grad[x, v] = before[z, x, v] + terms(e, turned, x, z, v)
            return 0

        lax.fori_loop(0, WIDTH, one, 0)
        copies.append(pltpu.make_async_copy(grads[away], grads_far[away], sems.at[away]))
        copies[-1].start()
    for copy in copies:
        copy.wait()


def sum_kernel(a, b, c, d, out):
    for x in range(WIDTH):
        for v in range(HALF):
            out[x, pl.ds(v, 8, stride=2), :] = (a[x, v] + b[x, v]) + (c[x, v] + d[x, v])


def add_kernel(*refs):
    total = refs[0][...]
    for ref in refs[1:-1]:
        total = total + ref[...]
    refs[-1][...] = total


def last_kernel(*refs):
    total = refs[0][...]
    for ref in refs[1:-1]:
        total = total + ref[...]
    lane = lax.broadcasted_iota(jnp.int32, (1, 128), 1)
    for f in range(FREQS):
        both = jnp.where(lane == 0, total[2 * f : 2 * f + 1], total[2 * f + 1 : 2 * f + 2])
        refs[-1][0, f : f + 1, :] = both[:, :2]


def f32(*shape):
    return jax.ShapeDtypeStruct(shape, jnp.float32)


VMEM = pl.BlockSpec(memory_space=pltpu.VMEM)
SMEM = pl.BlockSpec(memory_space=pltpu.SMEM)
FAR = pl.BlockSpec(memory_space=pltpu.HBM)
ANY = pl.BlockSpec(memory_space=pl.ANY)


def room(mib):
    return pltpu.CompilerParams(vmem_limit_bytes=mib * 1024 * 1024)


def held(*shape):
    return pltpu.VMEM(shape, jnp.float32)


def here(x):
    return pltpu.with_memory_space_constraint(x, pltpu.VMEM)


def far(x):
    return pltpu.with_memory_space_constraint(x, pltpu.HBM)


def body(e_start, h_start, forward, density, material, design, eps_table, profiles, port_mode):
    tiles = lax.axis_size("tile")
    ports = lax.axis_size("port")
    tile = lax.axis_index("tile")
    port = lax.axis_index("port")

    e_rows, h_rows = rows(e_start[0]), rows(h_start[0])
    planes = 2 * ROUND + DEPTH
    half = (3, WIDTH // 2 + 1) + CELLS

    def sent(count):
        return (pltpu.HBM((count, *CELLS), jnp.float32),) * 2

    info = jnp.stack([tile.astype(jnp.int32), port.astype(jnp.int32), port_mode[0]])
    coef, inter, intra = pl.pallas_call(
        free_kernel,
        out_shape=(f32(WIDTH, *CELLS),) + sent(planes),
        in_specs=[SMEM] * 2 + [FAR] * 5,
        out_specs=(VMEM,) + (FAR,) * 2,
        scratch_shapes=[held(*half)] * 4
        + [
            pltpu.VMEM((64, 16), jnp.int32),
            pltpu.VMEM((64, 16), jnp.int32),
            held(WIDTH, 64, 128),
            held(3, WIDTH, 64, 128),
            held(3, WIDTH, 64, 128),
            held(2, planes, *CELLS),
            pltpu.SemaphoreType.DMA((5,)),
            pltpu.SemaphoreType.DMA((4,)),
        ],
        compiler_params=room(12),
        name="free",
    )(
        info, far(eps_table), far(material.reshape(64, 16)), far(design.reshape(64, 16)), far(rows(density)),
        far(e_rows), far(h_rows),
    )
    across = [(i, i + 1) for i in range(1, tiles - 1, 2)]

    def swap(inter, intra):
        return (
            lax.ppermute(inter, "tile", across + [(j, i) for i, j in across]),
            lax.ppermute(intra, "tile", [(i, i ^ 1) for i in range(tiles)]),
        )

    blocks, inter, intra = lax.optimization_barrier((design.reshape(64, 16), inter, intra))
    inter, intra = swap(inter, intra)

    fields = held(3, WIDTH + 1, *CELLS)
    turned_shape = held(FREQS, 2, 3, SLAB, WIDTH, HALF, 8, 128)
    turned, profile, e_all, h_all = pl.pallas_call(
        wide_kernel,
        out_shape=(turned_shape, f32(64, 128), fields, fields),
        in_specs=[VMEM] * 5,
        out_specs=(VMEM,) * 4,
        scratch_shapes=[held(4 * 3, 64, 128), held(WIDTH, *CELLS)],
        compiler_params=room(4),
        name="wide",
    )(rows(forward[0]), blocks, rows(profiles), e_rows, h_rows)

    scale = 1.0 / math.sqrt(WIDTH * tiles * SLAB * 2048)
    edge = (3, DEPTH + 1) + CELLS
    history = held(ROUND, 3, WIDTH, *CELLS)
    halos = [
        held(3, DEPTH + 2, *CELLS),
        held(*edge),
        held(*edge),
        held(*edge),
        held(2, planes, *CELLS),
        pltpu.SemaphoreType.DMA((4,)),
    ]
    e_first, e_mid, h_mid, sums, late_inter, late_intra = pl.pallas_call(
        functools.partial(round_kernel, False, scale),
        out_shape=(history, fields, fields, f32(ROUND, HALF, 8, 128)) + sent(2 * ROUND),
        in_specs=[SMEM] + [VMEM] * 3 + [ANY] * 2,
        out_specs=(VMEM,) * 4 + (FAR,) * 2,
        scratch_shapes=halos
        + [held(*half)] * 4
        + [held(2, 2 * ROUND, *CELLS), pltpu.SemaphoreType.DMA((4,))],
        compiler_params=room(12),
        name="round",
    )(info, here(e_all), here(h_all), coef, inter, intra)
    late_inter, late_intra = swap(late_inter, late_intra)
    grad_first, turned = pl.pallas_call(
        first_kernel,
        out_shape=(f32(SLAB, WIDTH, HALF, 8, 128), turned_shape),
        in_specs=[VMEM] * 2,
        out_specs=(VMEM,) * 2,
        compiler_params=room(2),
        name="first",
    )(here(e_first), here(turned))
    sums, grad_first = lax.optimization_barrier((sums, grad_first))
    e_second, e_last, h_last, over = pl.pallas_call(
        functools.partial(round_kernel, True, scale),
        out_shape=(history, fields, fields, f32(2 * FREQS, 128)),
        in_specs=[SMEM] + [VMEM] * 3 + [ANY] * 4 + [VMEM] * 2,
        out_specs=(VMEM,) * 4,
        scratch_shapes=halos + [held(ROUND, HALF, 8, 128)],
        compiler_params=room(8),
        name="round",
    )(info, here(e_mid), here(h_mid), coef, inter, intra, late_inter, late_intra, profile, sums)
    parts = pl.pallas_call(
        finish_kernel,
        out_shape=(pltpu.HBM((WIDTH, HALF, 8, 128), jnp.float32),) * SLAB,
        in_specs=[SMEM] + [VMEM] * 3,
        out_specs=(FAR,) * SLAB,
        scratch_shapes=[held(WIDTH, HALF, 8, 128)] * SLAB + [pltpu.SemaphoreType.DMA((SLAB,))],
        compiler_params=room(4),
        name="finish",
    )(info, here(e_second), here(turned), grad_first)

    def to_port(x, d):
        return lax.ppermute(x, "port", [(i, (i + d) % ports) for i in range(ports)])

    def stage(total, steps, kernel=add_kernel, shape=(2 * FREQS, 128)):
        got = []
        for mask in range(1, 1 << len(steps)):
            flip = sum(by for bit, by in enumerate(steps) if mask >> bit & 1)
            got.append(lax.ppermute(total, "tile", [(i, i ^ flip) for i in range(tiles)]))
        return pl.pallas_call(
            kernel,
            out_shape=f32(*shape),
            in_specs=[VMEM] * (1 + len(got)),
            out_specs=VMEM,
            compiler_params=room(1),
            name="add",
        )(total, *got)

    e_out, h_out = pl.pallas_call(
        out_kernel,
        out_shape=(f32(3, WIDTH, 64, 128), f32(3, WIDTH, 64, 128)),
        in_specs=[VMEM] * 2,
        out_specs=(VMEM,) * 2,
        compiler_params=room(4),
        name="out",
    )(here(e_last), here(h_last))
    total = stage(over, (1, 8))
    total, *parts = lax.optimization_barrier((total, *parts))
    for d in range(1, ports):
        parts[d] = to_port(parts[d], d)
    total = stage(total, (2, 4))
    total, e_out, h_out, parts[1], parts[2] = lax.optimization_barrier((total, e_out, h_out, parts[1], parts[2]))
    intersections = stage(total, (16, 32), last_kernel, (1, FREQS, 2))
    gradient = pl.pallas_call(
        sum_kernel,
        out_shape=f32(WIDTH, 16, 128),
        in_specs=[VMEM] * 4,
        out_specs=VMEM,
        name="total",
    )(*parts)
    return (
        unrows(e_out)[None],
        unrows(h_out)[None],
        gradient.reshape(WIDTH, 1, 2048),
        intersections,
    )


def solution(mesh):
    return jax.shard_map(
        body,
        mesh=mesh,
        in_specs=(
            P("port", None, "tile", None, None),
            P("port", None, "tile", None, None),
            P("port", None, None, None, "tile", None, None),
            P("tile", None, None),
            P("tile", None, None),
            P("tile", None, None),
            P(),
            P(),
            P("port"),
        ),
        out_specs=(
            P("port", None, "tile", None, None),
            P("port", None, "tile", None, None),
            P("tile", "port", None),
            P("port", None, None),
        ),
        check_vma=False,
    )
```

```python
import functools
import math

import jax
import jax.numpy as jnp
import numpy as np
from jax import lax
from jax.experimental import pallas as pl
from jax.experimental.pallas import tpu as pltpu
from jax.sharding import PartitionSpec as P

STEPS = 16
OMEGA = 0.7
COEF_H = 0.5
COEF_E = 0.5

WIDTH = 16
SLAB = 4
HALF = 2
ROUND = STEPS // 2
DEPTH = ROUND // 2
FREQS = 2
CELLS = (SLAB, HALF, 8, 128)


def rows(x):
    lead = x.shape[:-2]
    x = x.reshape(lead + (SLAB, 16, 128))
    return jnp.swapaxes(x, -3, -2).reshape(lead + (64, 128))


def unrows(x):
    lead = x.shape[:-2]
    x = x.reshape(lead + (16, SLAB, 128))
    return jnp.swapaxes(x, -3, -2).reshape(lead + (SLAB, 2048))


def masks():
    lane = lax.broadcasted_iota(jnp.int32, (8, 128), 1)
    sub = lax.broadcasted_iota(jnp.int32, (8, 128), 0)
    return lane == 127, lane == 0, sub == 7, sub == 0


def ahead_y(pair, m):
    r0 = pltpu.roll(pair[0], 127, 1)
    r1 = pltpu.roll(pair[1], 127, 1)
    rs = jnp.where(m[2], 0.0, pltpu.roll(r0, 7, 0))
    return jnp.where(m[0], r1, r0), jnp.where(m[0], rs, r1)


def behind_y(pair, m):
    r0 = pltpu.roll(pair[0], 1, 1)
    r1 = pltpu.roll(pair[1], 1, 1)
    rs = jnp.where(m[3], 0.0, pltpu.roll(r1, 1, 0))
    return jnp.where(m[1], rs, r0), jnp.where(m[1], r0, r1)


def update_plane(e_old, e_next, h_now, h_prev, coef, e_new, m, keep=None, sums=None):
    def plane(ref, comp):
        return [[ref[comp, z, v] for v in range(HALF)] for z in range(SLAB)]

    ex, ey, ez = (plane(e_old, comp) for comp in range(3))
    ey_x, ez_x = plane(e_next, 1), plane(e_next, 2)
    hx, hy, hz = (plane(h_now, comp) for comp in range(3))
    hy_x, hz_x = plane(h_prev, 1), plane(h_prev, 2)
    c = [[coef[z, v] for v in range(HALF)] for z in range(SLAB)]
    edge = [0.0] * HALF
    new_e = []
    for z in range(SLAB):
        ex_z, ey_z = (ex[z + 1], ey[z + 1]) if z + 1 < SLAB else (edge, edge)
        ez_y, ex_y = ahead_y(ez[z], m), ahead_y(ex[z], m)
        for v in range(HALF):
            hx[z][v] = hx[z][v] - ((ez_y[v] - ez[z][v]) - (ey_z[v] - ey[z][v]))
            hy[z][v] = hy[z][v] - ((ex_z[v] - ex[z][v]) - (ez_x[z][v] - ez[z][v]))
            hz[z][v] = hz[z][v] - ((ey_x[z][v] - ey[z][v]) - (ex_y[v] - ex[z][v]))
        hz_y, hx_y = behind_y(hz[z], m), behind_y(hx[z], m)
        hx_z, hy_z = (hx[z - 1], hy[z - 1]) if z > 0 else (edge, edge)
        for v in range(HALF):
            curl_x = (hz[z][v] - hz_y[v]) - (hy[z][v] - hy_z[v])
            curl_y = (hx[z][v] - hx_z[v]) - (hz[z][v] - hz_x[z][v])
            curl_z = (hy[z][v] - hy_x[z][v]) - (hx[z][v] - hx_y[v])
            new_e.append(
                (
                    ex[z][v] + c[z][v] * curl_x,
                    ey[z][v] + c[z][v] * curl_y,
                    ez[z][v] + c[z][v] * curl_z,
                )
            )
    for z in range(SLAB):
        for v in range(HALF):
            for comp, h in enumerate((hx, hy, hz)):
                h_now[comp, z, v] = h[z][v]
                e_new[comp, z, v] = new_e[z * HALF + v][comp]
                if keep is not None:
                    keep[comp, z, v] = new_e[z * HALF + v][comp]
    if sums is not None:
        for v in range(HALF):
            sums[v] += sum(new_e[z * HALF + v][1] for z in range(SLAB))


def sweep(blocks, planes, one):
    def block(i, _):
        for plane in planes(i):
            one(plane)
        return 0

    lax.fori_loop(0, blocks, block, 0)


def strided(z, v):
    return pl.ds(4 * v + z, 8, stride=8)


def load_rows(src, dst, scale, first=0, count=WIDTH, base=0):
    def one(x, _):
        for comp in range(3):
            for z in range(SLAB):
                for v in range(HALF):
                    val = src[comp, first + x, strided(z, v), :]
                    dst[comp, base + x, z, v] = val if scale == 1.0 else val * scale
        return 0

    lax.fori_loop(0, count, one, 0)


def by_sublane(ref, v):
    row = lax.broadcasted_iota(jnp.int32, (8, 16), 0)
    col = lax.broadcasted_iota(jnp.int32, (8, 16), 1)
    pick = (col == HALF * row + v).astype(jnp.float32)
    values = ref[...].astype(jnp.float32)
    return lax.dot_general(pick, values, (((1,), (1,)), ((), ())), preferred_element_type=jnp.float32)


def free_run(ea, ha, eb, hb, coef, faces, sends):
    m = masks()
    half = WIDTH // 2
    to_left, to_right = faces.at[0], faces.at[1]
    for e, h in ((ea, ha), (eb, hb)):
        e[:, half] = jnp.zeros((3,) + CELLS, jnp.float32)
        h[:, 0] = jnp.zeros((3,) + CELLS, jnp.float32)

    def low(x):
        update_plane(ea.at[:, x], ea.at[:, x + 1], ha.at[:, x + 1], ha.at[:, x], coef.at[x], ea.at[:, x], m)

    def high(x):
        update_plane(eb.at[:, x], eb.at[:, x + 1], hb.at[:, x + 1], hb.at[:, x], coef.at[half + x], eb.at[:, x], m)

    def step(s, _):
        to_left[pl.ds(2 * s - 2, 2)] = ea[1:3, 0]
        blocks = (ROUND + 2 - s) // 2
        first = half - 2 * blocks
        sweep(
            blocks,
            lambda i: [(low, 2 * i), (high, first + 2 * i), (low, 2 * i + 1), (high, first + 2 * i + 1)],
            lambda job: job[0](job[1]),
        )
        to_right[pl.ds(2 * s - 2, 2)] = hb[1:3, half]
        return 0

    lax.fori_loop(1, ROUND // 2 + 1, step, 0)
    for copy in sends[:2]:
        copy.start()
    lax.fori_loop(ROUND // 2 + 1, ROUND + 1, step, 0)
    for copy in sends[2:]:
        copy.start()
    for copy in sends:
        copy.wait()


def swaps(info, faces, inter_far, intra_far, sems):
    odd = lax.rem(info[0], 2)
    copies = []
    for part in (pl.ds(0, ROUND), pl.ds(ROUND, faces.shape[1] - ROUND)):
        for side, far in ((odd, inter_far), (1 - odd, intra_far)):
            copies.append(pltpu.make_async_copy(faces.at[side, part], far.at[part], sems.at[len(copies)]))
    return copies


def free_kernel(
    info, table, mat_far, des_far, dens_far, e_far, h_far,
    coef, inter_far, intra_far,
    ea, ha, eb, hb, mat, des, dens, e_in, h_in, faces, sems, sent,
):
    to_left, to_right = faces.at[0], faces.at[1]
    pairs = ((mat_far, mat), (des_far, des), (dens_far, dens), (e_far, e_in), (h_far, h_in))
    fetch = [pltpu.make_async_copy(src, dst, sems.at[i]) for i, (src, dst) in enumerate(pairs)]
    for copy in fetch:
        copy.start()
    for copy in fetch[:3]:
        copy.wait()
    for v in range(HALF):
        kind = by_sublane(mat, v)
        flag = by_sublane(des, v)
        base = jnp.zeros(kind.shape, jnp.float32)
        for which in range(table.shape[0]):
            base = base + jnp.where(kind == which, table[which], 0.0)
        for x in range(WIDTH):
            for z in range(SLAB):
                at = x * SLAB + z
                b = jnp.broadcast_to(base[:, at : at + 1], (8, 128))
                d = jnp.broadcast_to(flag[:, at : at + 1], (8, 128))
                eps = b + d * dens[x, strided(z, v), :]
                coef[x, z, v] = (COEF_E * COEF_H) / eps
    to_left[2 * ROUND :] = coef[:DEPTH]
    to_right[2 * ROUND :] = coef[WIDTH - DEPTH :]

    half = WIDTH // 2
    fetch[3].wait()
    load_rows(e_in, ea, 1.0, 0, half)
    load_rows(e_in, eb, 1.0, half, half)
    fetch[4].wait()
    load_rows(h_in, ha, 1.0 / COEF_H, 0, half, 1)
    load_rows(h_in, hb, 1.0 / COEF_H, half, half, 1)
    free_run(ea, ha, eb, hb, coef, faces, swaps(info, faces, inter_far, intra_far, sent))


def angles():
    omegas = [OMEGA * (f + 1) for f in range(FREQS)]
    mid = (ROUND + 1) / 2
    return omegas, [float(np.cos(w * mid)) for w in omegas], [float(np.sin(w * mid)) for w in omegas]


def wide_kernel(forward, des, profile_in, e_in, h_in, turned, profile, e_all, h_all, wide, mask):
    _, ca, sa = angles()
    profile[...] = profile_in[...]
    for v in range(HALF):
        flag = by_sublane(des, v)
        for x in range(WIDTH):
            for z in range(SLAB):
                at = x * SLAB + z
                mask[x, z, v] = jnp.broadcast_to(flag[:, at : at + 1], (8, 128)) * (1.0 / STEPS)
    load_rows(e_in, e_all, 1.0)
    load_rows(h_in, h_all, 1.0 / COEF_H, base=1)

    def one(x, _):
        for f in range(FREQS):
            for q in range(2):
                for comp in range(3):
                    wide[(f * 2 + q) * 3 + comp] = forward[f, q, comp, x].astype(jnp.float32)

        def at_z(z, _):
            for v in range(HALF):
                keep = mask[x, z, v]
                for f in range(FREQS):
                    for comp in range(3):
                        re = wide[(f * 2) * 3 + comp, strided(z, v), :]
                        im = wide[(f * 2 + 1) * 3 + comp, strided(z, v), :]
                        turned[f, 0, comp, z, x, v] = keep * (re * ca[f] + im * sa[f])
                        turned[f, 1, comp, z, x, v] = keep * (im * ca[f] - re * sa[f])
            return 0

        return lax.fori_loop(0, SLAB, at_z, 0)

    lax.fori_loop(0, WIDTH, one, 0)


def terms(e, turned, x, z, v):
    omegas, _, _ = angles()
    total = None
    for comp in range(3):
        plus, minus = [], []
        for i in range(ROUND // 2):
            lo = e[ROUND // 2 - 1 - i, comp, x, z, v]
            hi = e[ROUND // 2 + i, comp, x, z, v]
            plus.append(hi + lo)
            minus.append(hi - lo)
        for f in range(FREQS):
            even = odd = None
            for i in range(ROUND // 2):
                c = float(np.cos(omegas[f] * (i + 0.5)))
                s = float(np.sin(omegas[f] * (i + 0.5)))
                even = c * plus[i] if even is None else even + c * plus[i]
                odd = s * minus[i] if odd is None else odd + s * minus[i]
            term = even * turned[f, 0, comp, z, x, v] + odd * turned[f, 1, comp, z, x, v]
            total = term if total is None else total + term
    return total


def first_kernel(e, turned, grad, later):
    omegas, _, _ = angles()

    def one(x, _):
        def at_z(z, _):
            for v in range(HALF):
                grad[z, x, v] = terms(e, turned, x, z, v)
                for f in range(FREQS):
                    c, s = float(np.cos(omegas[f] * ROUND)), float(np.sin(omegas[f] * ROUND))
                    for comp in range(3):
                        re, im = turned[f, 0, comp, z, x, v], turned[f, 1, comp, z, x, v]
                        later[f, 0, comp, z, x, v] = c * re + s * im
                        later[f, 1, comp, z, x, v] = c * im - s * re
            return 0

        return lax.fori_loop(0, SLAB, at_z, 0)

    lax.fori_loop(0, WIDTH, one, 0)


def out_kernel(e, h, e_out, h_out):
    def one(x, _):
        for z in range(SLAB):
            for v in range(HALF):
                for comp in range(3):
                    e_out[comp, x, strided(z, v), :] = e[comp, x, z, v]
                    h_out[comp, x, strided(z, v), :] = h[comp, x + 1, z, v] * COEF_H
        return 0

    lax.fori_loop(0, WIDTH, one, 0)


def round_kernel(final, scale, info, e_in, h_in, coef, inter, intra, *rest):
    if final:
        (late_inter, late_intra, profile, sums_before), rest = rest[:4], rest[4:]
        (e, now, h, over), (el, hl, er, hr, got, sems, sums) = rest[:4], rest[4:]
    else:
        (e, now, h, sums, inter_far, intra_far), rest = rest[:6], rest[6:]
        el, hl, er, hr, got, sems, ea, ha, eb, hb, faces, sent = rest
        late_inter, late_intra = inter, intra
    m = masks()
    odd = lax.rem(info[0], 2)
    hist, tail = pl.ds(0, 2 * ROUND), pl.ds(2 * ROUND, DEPTH)
    fetch = []
    for side, early, late in ((odd, inter, late_inter), (1 - odd, intra, late_intra)):
        for src, part in ((late, hist), (early, tail)):
            fetch.append(pltpu.make_async_copy(src.at[part], got.at[side, part], sems.at[len(fetch)]))
    for copy in fetch:
        copy.start()
    from_left, from_right = got.at[0], got.at[1]

    def place(x, _):
        for comp in range(3):
            now[comp, x] = e_in[comp, x]
            h[comp, x + 1] = h_in[comp, x + 1]
        return 0

    lax.fori_loop(0, WIDTH, place, 0)
    sums[...] = jnp.zeros(sums.shape, jnp.float32)
    for ref in (el, hl, er, hr):
        ref[...] = jnp.zeros(ref.shape, jnp.float32)
    inner = (info[0] > 0).astype(jnp.float32)

    def left(x):
        update_plane(
            el.at[:, x + 1], el.at[:, x + 2], hl.at[:, x + 1], hl.at[:, x],
            from_left.at[2 * ROUND + x], el.at[:, x + 1], m,
        )

    def right(x):
        update_plane(
            er.at[:, x], er.at[:, x + 1], hr.at[:, x + 1], hr.at[:, x],
            from_right.at[2 * ROUND + x], er.at[:, x], m,
        )

    def halos(s):
        el[1:3, DEPTH + 1] = now[1:3, 0]
        blocks = (jnp.minimum(s + 1, ROUND - s) + 1) // 2
        low = DEPTH - 2 * blocks
        sweep(
            blocks,
            lambda i: [(left, low + 2 * i), (right, 2 * i), (left, low + 2 * i + 1), (right, 2 * i + 1)],
            lambda job: job[0](job[1]),
        )

    def step(s, _):
        now[1:3, WIDTH] = er[1:3, 0] + from_right[pl.ds(2 * s - 2, 2)]
        h[1:3, 0] = hl[1:3, DEPTH] * inner + from_left[pl.ds(2 * s - 2, 2)]

        def own(x):
            update_plane(
                now.at[:, x], now.at[:, x + 1], h.at[:, x + 1], h.at[:, x], coef.at[x], now.at[:, x], m,
                e.at[s - 1, :, x], sums.at[s - 1],
            )

        sweep(WIDTH // 4, lambda i: [4 * i + k for k in range(4)], own)
        hr[1:3, 0] = h[1:3, WIDTH]
        halos(s)
        return 0

    for copy in fetch:
        copy.wait()
    halos(0)
    lax.fori_loop(1, ROUND + 1, step, 0)

    if not final:
        half = WIDTH // 2

        def split(x, _):
            for comp in range(3):
                ea[comp, x] = now[comp, x]
                eb[comp, x] = now[comp, half + x]
                ha[comp, x + 1] = h[comp, x + 1]
                hb[comp, x + 1] = h[comp, half + x + 1]
            return 0

        lax.fori_loop(0, half, split, 0)
        free_run(ea, ha, eb, hb, coef, faces, swaps(info, faces, inter_far, intra_far, sent))
        return

    omegas, _, _ = angles()
    profiled = [
        sum(ref[t, v] * profile[strided(info[2], v), :] for v in range(HALF))
        for ref in (sums_before, sums)
        for t in range(ROUND)
    ]
    for f in range(FREQS):
        for q, turn in enumerate((np.cos, lambda angle: -np.sin(angle))):
            val = sum(float(turn(omegas[f] * (t + 1))) * profiled[t] for t in range(STEPS))
            val = jnp.sum(jnp.sum(val, axis=0, keepdims=True), axis=1, keepdims=True)
            over[2 * f + q : 2 * f + q + 1, :] = jnp.broadcast_to(val * scale, (1, 128))


def finish_kernel(info, e, turned, before, g0, g1, g2, g3, *scratch):
    grads_far, (*grads, sems) = (g0, g1, g2, g3), scratch
    copies = []
    for away in (1, 2, 3, 0):
        z = lax.rem(info[1] + away, SLAB)

        def one(x, _, grad=grads[away], z=z):
            for v in range(HALF):
                grad[x, v] = before[z, x, v] + terms(e, turned, x, z, v)
            return 0

        lax.fori_loop(0, WIDTH, one, 0)
        copies.append(pltpu.make_async_copy(grads[away], grads_far[away], sems.at[away]))
        copies[-1].start()
    for copy in copies:
        copy.wait()


def sum_kernel(a, b, c, d, out):
    for x in range(WIDTH):
        for v in range(HALF):
            out[x, pl.ds(v, 8, stride=2), :] = (a[x, v] + b[x, v]) + (c[x, v] + d[x, v])


def add_kernel(*refs):
    total = refs[0][...]
    for ref in refs[1:-1]:
        total = total + ref[...]
    refs[-1][...] = total


def last_kernel(*refs):
    total = refs[0][...]
    for ref in refs[1:-1]:
        total = total + ref[...]
    lane = lax.broadcasted_iota(jnp.int32, (1, 128), 1)
    for f in range(FREQS):
        both = jnp.where(lane == 0, total[2 * f : 2 * f + 1], total[2 * f + 1 : 2 * f + 2])
        refs[-1][0, f : f + 1, :] = both[:, :2]


def f32(*shape):
    return jax.ShapeDtypeStruct(shape, jnp.float32)


VMEM = pl.BlockSpec(memory_space=pltpu.VMEM)
SMEM = pl.BlockSpec(memory_space=pltpu.SMEM)
FAR = pl.BlockSpec(memory_space=pltpu.HBM)
ANY = pl.BlockSpec(memory_space=pl.ANY)


def room(mib):
    return pltpu.CompilerParams(vmem_limit_bytes=mib * 1024 * 1024)


def held(*shape):
    return pltpu.VMEM(shape, jnp.float32)


def here(x):
    return pltpu.with_memory_space_constraint(x, pltpu.VMEM)


def far(x):
    return pltpu.with_memory_space_constraint(x, pltpu.HBM)


def body(e_start, h_start, forward, density, material, design, eps_table, profiles, port_mode):
    tiles = lax.axis_size("tile")
    ports = lax.axis_size("port")
    tile = lax.axis_index("tile")
    port = lax.axis_index("port")

    e_rows, h_rows = rows(e_start[0]), rows(h_start[0])
    planes = 2 * ROUND + DEPTH
    half = (3, WIDTH // 2 + 1) + CELLS

    def sent(count):
        return (pltpu.HBM((count, *CELLS), jnp.float32),) * 2

    info = jnp.stack([tile.astype(jnp.int32), port.astype(jnp.int32), port_mode[0]])
    coef, inter, intra = pl.pallas_call(
        free_kernel,
        out_shape=(f32(WIDTH, *CELLS),) + sent(planes),
        in_specs=[SMEM] * 2 + [FAR] * 5,
        out_specs=(VMEM,) + (FAR,) * 2,
        scratch_shapes=[held(*half)] * 4
        + [
            pltpu.VMEM((64, 16), jnp.int32),
            pltpu.VMEM((64, 16), jnp.int32),
            held(WIDTH, 64, 128),
            held(3, WIDTH, 64, 128),
            held(3, WIDTH, 64, 128),
            held(2, planes, *CELLS),
            pltpu.SemaphoreType.DMA((5,)),
            pltpu.SemaphoreType.DMA((4,)),
        ],
        compiler_params=room(12),
        name="free",
    )(
        info, far(eps_table), far(material.reshape(64, 16)), far(design.reshape(64, 16)), far(rows(density)),
        far(e_rows), far(h_rows),
    )
    across = [(i, i + 1) for i in range(1, tiles - 1, 2)]

    def swap(inter, intra):
        return (
            lax.ppermute(inter, "tile", across + [(j, i) for i, j in across]),
            lax.ppermute(intra, "tile", [(i, i ^ 1) for i in range(tiles)]),
        )

    blocks, inter, intra = lax.optimization_barrier((design.reshape(64, 16), inter, intra))
    inter, intra = swap(inter, intra)

    fields = held(3, WIDTH + 1, *CELLS)
    turned_shape = held(FREQS, 2, 3, SLAB, WIDTH, HALF, 8, 128)
    turned, profile, e_all, h_all = pl.pallas_call(
        wide_kernel,
        out_shape=(turned_shape, f32(64, 128), fields, fields),
        in_specs=[VMEM] * 5,
        out_specs=(VMEM,) * 4,
        scratch_shapes=[held(4 * 3, 64, 128), held(WIDTH, *CELLS)],
        compiler_params=room(4),
        name="wide",
    )(rows(forward[0]), blocks, rows(profiles), e_rows, h_rows)

    scale = 1.0 / math.sqrt(WIDTH * tiles * SLAB * 2048)
    edge = (3, DEPTH + 1) + CELLS
    history = held(ROUND, 3, WIDTH, *CELLS)
    halos = [
        held(3, DEPTH + 2, *CELLS),
        held(*edge),
        held(*edge),
        held(*edge),
        held(2, planes, *CELLS),
        pltpu.SemaphoreType.DMA((4,)),
    ]
    e_first, e_mid, h_mid, sums, late_inter, late_intra = pl.pallas_call(
        functools.partial(round_kernel, False, scale),
        out_shape=(history, fields, fields, f32(ROUND, HALF, 8, 128)) + sent(2 * ROUND),
        in_specs=[SMEM] + [VMEM] * 3 + [ANY] * 2,
        out_specs=(VMEM,) * 4 + (FAR,) * 2,
        scratch_shapes=halos
        + [held(*half)] * 4
        + [held(2, 2 * ROUND, *CELLS), pltpu.SemaphoreType.DMA((4,))],
        compiler_params=room(12),
        name="round",
    )(info, here(e_all), here(h_all), coef, inter, intra)
    late_inter, late_intra = swap(late_inter, late_intra)
    grad_first, turned = pl.pallas_call(
        first_kernel,
        out_shape=(f32(SLAB, WIDTH, HALF, 8, 128), turned_shape),
        in_specs=[VMEM] * 2,
        out_specs=(VMEM,) * 2,
        compiler_params=room(2),
        name="first",
    )(here(e_first), here(turned))
    sums, grad_first = lax.optimization_barrier((sums, grad_first))
    e_second, e_last, h_last, over = pl.pallas_call(
        functools.partial(round_kernel, True, scale),
        out_shape=(history, fields, fields, f32(2 * FREQS, 128)),
        in_specs=[SMEM] + [VMEM] * 3 + [ANY] * 4 + [VMEM] * 2,
        out_specs=(VMEM,) * 4,
        scratch_shapes=halos + [held(ROUND, HALF, 8, 128)],
        compiler_params=room(8),
        name="round",
    )(info, here(e_mid), here(h_mid), coef, inter, intra, late_inter, late_intra, profile, sums)
    parts = pl.pallas_call(
        finish_kernel,
        out_shape=(pltpu.HBM((WIDTH, HALF, 8, 128), jnp.float32),) * SLAB,
        in_specs=[SMEM] + [VMEM] * 3,
        out_specs=(FAR,) * SLAB,
        scratch_shapes=[held(WIDTH, HALF, 8, 128)] * SLAB + [pltpu.SemaphoreType.DMA((SLAB,))],
        compiler_params=room(4),
        name="finish",
    )(info, here(e_second), here(turned), grad_first)

    def to_port(x, d):
        return lax.ppermute(x, "port", [(i, (i + d) % ports) for i in range(ports)])

    def stage(total, steps, kernel=add_kernel, shape=(2 * FREQS, 128)):
        got = []
        for mask in range(1, 1 << len(steps)):
            flip = sum(by for bit, by in enumerate(steps) if mask >> bit & 1)
            got.append(lax.ppermute(total, "tile", [(i, i ^ flip) for i in range(tiles)]))
        return pl.pallas_call(
            kernel,
            out_shape=f32(*shape),
            in_specs=[VMEM] * (1 + len(got)),
            out_specs=VMEM,
            compiler_params=room(1),
            name="add",
        )(total, *got)

    e_out, h_out = pl.pallas_call(
        out_kernel,
        out_shape=(f32(3, WIDTH, 64, 128), f32(3, WIDTH, 64, 128)),
        in_specs=[VMEM] * 2,
        out_specs=(VMEM,) * 2,
        compiler_params=room(4),
        name="out",
    )(here(e_last), here(h_last))
    total = stage(over, (1, 8))
    total, *parts = lax.optimization_barrier((total, *parts))
    for d in (2, 1, 3):
        parts[d] = to_port(parts[d], d)
    total = stage(total, (2, 4))
    total, e_out, h_out, parts[1], parts[2] = lax.optimization_barrier((total, e_out, h_out, parts[1], parts[2]))
    intersections = stage(total, (16, 32), last_kernel, (1, FREQS, 2))
    gradient = pl.pallas_call(
        sum_kernel,
        out_shape=f32(WIDTH, 16, 128),
        in_specs=[VMEM] * 4,
        out_specs=VMEM,
        name="total",
    )(*parts)
    return (
        unrows(e_out)[None],
        unrows(h_out)[None],
        gradient.reshape(WIDTH, 1, 2048),
        intersections,
    )


def solution(mesh):
    return jax.shard_map(
        body,
        mesh=mesh,
        in_specs=(
            P("port", None, "tile", None, None),
            P("port", None, "tile", None, None),
            P("port", None, None, None, "tile", None, None),
            P("tile", None, None),
            P("tile", None, None),
            P("tile", None, None),
            P(),
            P(),
            P("port"),
        ),
        out_specs=(
            P("port", None, "tile", None, None),
            P("port", None, "tile", None, None),
            P("tile", "port", None),
            P("port", None, None),
        ),
        check_vma=False,
    )
```
